128 devices in a mesh: section: 4 (over y), seq: 32 (over x, z, core).
Axes of the slice: x: 4, y: 4, z: 4, core: 2. Of those that a mesh axis runs over, the one named last changes fastest.
Arguments:
- tokens: bfloat16 [1, 4096, 2560], P(None, 'seq'), may hold values from -7 to 7
- w_qkv: bfloat16 [4, 2560, 3840], P('section', 'seq')
- w_out: bfloat16 [4, 1280, 2560], P('section', 'seq'), may hold values from -0.15625 to 0.15625
- offsets: int32 [4, 10], replicated, may hold values from 0 to 7, as said below
Outputs:
- layer_outputs: bfloat16 [4, 1, 4096, 2560], P('section', None, 'seq')
The draws below stay inside these ranges and needn't reach their ends.
Inputs may be any that keep to these rules, and one draw needn't show every extreme that they name: offsets[b, h] lies below 2^b, and for each b every value below 2^b is taken by some head.
All inputs are finite; a program needn't handle non-finite values.
Results may differ from the reference program's by a relative error of at most 0.035.
Values may be sent and summed in bfloat16 or wider, within the bound.
No kernel may reach another device: no remote copies, remote signals or barrier semaphores. Data moves between devices by JAX's collectives and lax.ppermute only.
A program may use at most 128 MiB of HBM per device.

```python
import math
import jax
import jax.numpy as jnp
from jax import lax

D = 2560
HEADS = 10
HD = 128
BRANCHES = 4
TOK_DEV = 128
MICRO = 1
LAYERS = 4
SEQLEN = 4096


def draw_tokens(key, part):
    key = jax.random.fold_in(key, 2)
    first_key = jax.random.fold_in(key, 0)
    values = jnp.clip(jax.random.normal(first_key, (MICRO, SEQLEN, D), jnp.float32), -6.0, 6.0)
    return values.astype(jnp.bfloat16)


def draw_w_qkv(key, part):
    key = jax.random.fold_in(key, 3)
    first_key, second_key, third_key = jax.random.split(key, 3)
    mixing = 0.2
    shape = (LAYERS, D, HEADS * HD)
    query_part = jnp.clip(jax.random.normal(first_key, shape, jnp.float32), -4.0, 4.0)
    own_part = jnp.clip(jax.random.normal(second_key, shape, jnp.float32), -4.0, 4.0)
    value_part = jnp.clip(jax.random.normal(third_key, shape, jnp.float32), -4.0, 4.0)
    key_part = mixing * query_part + math.sqrt(1.0 - mixing * mixing) * own_part
    joined = jnp.concatenate([query_part, key_part, value_part], axis=2) / math.sqrt(D)
    return joined.astype(jnp.bfloat16)


def draw_offsets(key, part):
    key = jax.random.fold_in(key, 5)
    shift_key, order_key = jax.random.split(key)
    group_sizes = (2 ** jnp.arange(BRANCHES)).astype(jnp.int32)
    shifts = jax.random.randint(shift_key, (BRANCHES, 1), 0, 2 ** (BRANCHES - 1)).astype(jnp.int32)
    order_keys = jax.random.split(order_key, BRANCHES)
    orders = jax.vmap(lambda each_key: jax.random.permutation(each_key, HEADS))(order_keys).astype(jnp.int32)
    return ((orders + shifts) % group_sizes[:, None]).astype(jnp.int32)


def levels(key, dims, cuts, smallest, high):
    def one(axis_at, shards_of):
        heights = jax.random.uniform(jax.random.fold_in(jax.random.fold_in(key, 6), axis_at), (shards_of,), jnp.float32, smallest / len(cuts), high / len(cuts))
        return jnp.repeat(jnp.exp(heights), dims[axis_at] // shards_of).reshape((-1,) + (1,) * (len(dims) - axis_at - 1))

    factor_of = one(*cuts[0])
    for cut in cuts[1:]:
        factor_of = factor_of * one(*cut)
    return factor_of


def noise(rng, dims, spread, most, cuts=(), kind=jnp.bfloat16):
    array = spread * jax.random.normal(rng, dims, jnp.float32)
    if cuts:
        array = array * levels(rng, dims, cuts, -0.22, 0.18)
    return jnp.clip(array, -most, most).astype(kind)


def setup_inputs(seed: int = 0) -> dict:
    arg_keys = jax.random.split(jax.random.key(seed), 5)
    tokens = draw_tokens(jax.random.fold_in(arg_keys[4], 71), 0)
    w_qkv = draw_w_qkv(jax.random.fold_in(arg_keys[4], 71), 0)
    w_out = noise(arg_keys[2], (LAYERS, HEADS * HD, D), (HEADS * HD) ** -0.5, 0.15625, ((0, 4), (1, 32)))
    offsets = draw_offsets(jax.random.fold_in(arg_keys[4], 71), 0)
    return dict(tokens=tokens, w_qkv=w_qkv, w_out=w_out, offsets=offsets)


NEG_FILL = -1e+30

def branch_reference(query_all, key_all, value_all, offset_row, group_size):
    seq_len, head_count, head_dim = query_all.shape
    seg_count = seq_len // (group_size * TOK_DEV)
    present = jnp.arange(group_size)[:, None] == offset_row[None, :]

    def pick(source):
        shaped = source.reshape(seg_count, TOK_DEV, group_size, head_count, head_dim)
        return lax.optimization_barrier(jnp.sum(jnp.where(present[None, None, :, :, None], shaped, jnp.zeros((), source.dtype)), axis=2))
    query = pick(query_all)
    key_rows = pick(key_all)
    value_rows = pick(value_all)
    scaling = 1.0 / math.sqrt(head_dim)
    scores = jnp.einsum('nqhd,nkhd->nhqk', query.astype(jnp.float32), key_rows.astype(jnp.float32)) * scaling
    allowed = jnp.tril(jnp.ones((TOK_DEV, TOK_DEV), dtype=bool))[None, None]
    scores = jnp.where(allowed, scores, NEG_FILL)
    peak = lax.optimization_barrier(jnp.max(scores, axis=3))
    expos = jnp.where(allowed, jnp.exp(scores - peak[..., None]), 0.0)
    denominator = lax.optimization_barrier(jnp.sum(expos, axis=3))
    probs = expos.astype(jnp.bfloat16)
    mixed = jnp.einsum('nhqk,nkhd->nqhd', probs.astype(jnp.float32), value_rows.astype(jnp.float32))
    mixed = mixed / jnp.transpose(denominator, (0, 2, 1))[..., None]
    log_sum = jnp.transpose(peak + jnp.log(denominator), (0, 2, 1))
    full = jnp.where(present[None, None, :, :, None], mixed[:, :, None], 0.0).reshape(seq_len, head_count, head_dim)
    lse_full = jnp.where(present[None, None], log_sum[:, :, None], NEG_FILL).reshape(seq_len, head_count)
    return (full, lse_full)

def layer_reference(inputs, w_in, w_back, offsets):
    seq_len = inputs.shape[0]
    head_count = offsets.shape[1]
    head_dim = w_in.shape[1] // (3 * head_count)
    projected = jnp.dot(inputs, w_in, preferred_element_type=jnp.float32).astype(jnp.bfloat16)
    projected = projected.reshape(seq_len, 3, head_count, head_dim)
    outs_list = []
    lse_list = []
    for branch in range(BRANCHES):
        full, lse_full = branch_reference(projected[:, 0], projected[:, 1], projected[:, 2], offsets[branch], 2 ** branch)
        outs_list.append(full)
        lse_list.append(lse_full)
    stacked_lse = jnp.stack(lse_list)
    peak = lax.optimization_barrier(jnp.max(stacked_lse, axis=0))
    weights = jnp.exp(stacked_lse - peak[None])
    attended = lax.optimization_barrier(jnp.sum(weights[..., None] * jnp.stack(outs_list), axis=0)) / lax.optimization_barrier(jnp.sum(weights, axis=0))[..., None]
    attended = attended.astype(jnp.bfloat16).reshape(seq_len, head_count * head_dim)
    result = inputs.astype(jnp.float32) + jnp.dot(attended, w_back, preferred_element_type=jnp.float32)
    return result.astype(jnp.bfloat16)

def reference(tokens, w_qkv, w_out, offsets):
    carried = [tokens[slot] for slot in range(MICRO)]
    layer_list = []
    for layer_id in range(LAYERS):
        carried = [layer_reference(carried[slot], w_qkv[layer_id], w_out[layer_id], offsets) for slot in range(MICRO)]
        layer_list.append(jnp.stack(carried))
    return jnp.stack(layer_list)
```

```python
import functools
import math

import jax
import jax.numpy as jnp
from jax import lax
from jax.experimental import pallas as pl
from jax.experimental.pallas import tpu as pltpu
from jax.sharding import PartitionSpec as P

NEG_FILL = -1e30
HD = 128
CHIP_ROWS = 256
GROUP_CHIPS = 4
BF16 = jnp.bfloat16
F32 = jnp.float32
VMEM_LIMIT = 32 * 1024 * 1024


def dot(a, b):
    return lax.dot_general(a, b, (((1,), (0,)), ((), ())), preferred_element_type=F32)


def dot_t(a, b):
    return lax.dot_general(a, b, (((1,), (1,)), ((), ())), preferred_element_type=F32)


def offset_of(scalars, branch, head_at, heads):
    return scalars[2 + branch * 2 * heads + scalars[0] * heads + head_at]


def kv_kernel(heads, scalars, x_own, x_other, w, kv_out, send_out, acc):
    half = pl.program_id(1)

    @pl.when(half == 0)
    def _():
        acc[...] = dot(x_own[...], w[...])

    @pl.when(half == 1)
    def _():
        rows = (acc[...] + dot(x_other[...], w[...])).astype(BF16)
        kv_out[...] = rows
        row = lax.broadcasted_iota(jnp.int32, (96, CHIP_ROWS), 0)
        col = lax.broadcasted_iota(jnp.int32, (96, CHIP_ROWS), 1)
        for i in range(heads):
            off2 = offset_of(scalars, 2, i, heads)
            off3 = offset_of(scalars, 3, i, heads)
            source = jnp.where(row < 64, 4 * row + off2, 8 * (row - 64) + off3)
            pick = jnp.where(col == source, 1.0, 0.0).astype(BF16)
            cols = slice(i * HD, (i + 1) * HD)
            send_out[:, cols] = dot(pick, rows[:, cols]).astype(BF16)


def local_kernel(heads, scalars, x_own, x_other, w, kv, q_out, acc_out, stat_out, acc):
    half = pl.program_id(0)

    @pl.when(half == 0)
    def _():
        acc[...] = dot(x_own[...], w[...])

    @pl.when(half == 1)
    def _():
        query = (acc[...] + dot(x_other[...], w[...])).astype(BF16)
        q_out[...] = query
        scaling = 1.0 / math.sqrt(HD)
        shape = (CHIP_ROWS, CHIP_ROWS)
        causal = lax.broadcasted_iota(jnp.int32, shape, 1) <= lax.broadcasted_iota(
            jnp.int32, shape, 0
        )
        row = lax.broadcasted_iota(jnp.int32, (CHIP_ROWS, HD), 0)
        lane = lax.broadcasted_iota(jnp.int32, (CHIP_ROWS, HD), 1)
        first = ((lane == 0) & (row < 128)) | ((lane == 1) & (row >= 128))
        period = jnp.where(lane == 2, 1, jnp.where(lane == 3, 3, 7))
        in_branch = (lane >= 2) & (lane <= 4)
        stats = jnp.zeros((CHIP_ROWS, HD), F32)
        width = heads * HD
        for i in range(heads):
            cols = slice(i * HD, (i + 1) * HD)
            offset = jnp.where(
                lane == 2,
                offset_of(scalars, 1, i, heads),
                jnp.where(
                    lane == 3, offset_of(scalars, 2, i, heads), offset_of(scalars, 3, i, heads)
                ),
            )
            member = first | (in_branch & ((row & period) == offset))
            member = jnp.where(member, 1.0, 0.0).astype(BF16)
            times = jnp.where(causal, dot_t(member, member), 0.0)
            scores = dot_t(query[:, cols], kv[:, cols]) * scaling
            scores = jnp.where(times > 0.0, scores, NEG_FILL)
            peak = jnp.max(scores, axis=1, keepdims=True)
            expos = times * jnp.exp(scores - peak)
            total = jnp.sum(expos, axis=1, keepdims=True)
            acc_out[:, cols] = dot(
                expos.astype(BF16), kv[:, width + i * HD : width + (i + 1) * HD]
            )
            stats = jnp.where(lane == i, peak, jnp.where(lane == heads + i, total, stats))
        stat_out[...] = stats


def remote_kernel(heads, scalars, query, acc, stats, near, mid, far, out):
    scaling = 1.0 / math.sqrt(HD)
    chip = scalars[1]
    width = heads * HD
    keys = 160
    row = lax.broadcasted_iota(jnp.int32, (CHIP_ROWS, keys), 0)
    col = lax.broadcasted_iota(jnp.int32, (CHIP_ROWS, keys), 1)
    second = (col < 64) & ((chip & 1) == 1)
    third = (col >= 64) & (chip >= 1 + (col - 64) // 32)
    stat = stats[...]
    for i in range(heads):
        cols = slice(i * HD, (i + 1) * HD)
        vals = slice(width + i * HD, width + (i + 1) * HD)
        off2 = offset_of(scalars, 2, i, heads)
        off3 = offset_of(scalars, 3, i, heads)
        allowed = (second & ((row & 3) == off2)) | (third & ((row & 7) == off3))
        key_rows = jnp.concatenate([near[:, cols], mid[:, cols], far[:, cols]], axis=0)
        value_rows = jnp.concatenate([near[:, vals], mid[:, vals], far[:, vals]], axis=0)
        scores = dot_t(query[:, cols], key_rows) * scaling
        scores = jnp.where(allowed, scores, NEG_FILL)
        peak = stat[:, i : i + 1]
        total = stat[:, heads + i : heads + i + 1]
        new_peak = jnp.maximum(peak, jnp.max(scores, axis=1, keepdims=True))
        expos = jnp.exp(scores - new_peak)
        shrink = jnp.exp(peak - new_peak)
        total = total * shrink + jnp.sum(expos, axis=1, keepdims=True)
        mixed = acc[:, cols] * shrink + dot(expos.astype(BF16), value_rows)
        out[:, cols] = (mixed / total).astype(BF16)


def back_kernel(scalars, x_own, att_own, att_other, w, out, acc):
    half = pl.program_id(0)

    @pl.when(half == 0)
    def _():
        acc[...] = x_own[...].astype(F32) + dot(att_own[...], w[...])

    @pl.when(half == 1)
    def _():
        out[...] = (acc[...] + dot(att_other[...], w[...])).astype(BF16)


def call(body, grid, in_specs, out_specs, out_shape, scratch, flops, moved):
    return pl.pallas_call(
        body,
        grid_spec=pltpu.PrefetchScalarGridSpec(
            num_scalar_prefetch=1,
            grid=grid,
            in_specs=in_specs,
            out_specs=out_specs,
            scratch_shapes=scratch,
        ),
        out_shape=out_shape,
        compiler_params=pltpu.CompilerParams(vmem_limit_bytes=VMEM_LIMIT),
        cost_estimate=pl.CostEstimate(flops=flops, bytes_accessed=moved, transcendentals=0),
    )


def whole(shape):
    return pl.BlockSpec(shape, lambda *_: (0,) * len(shape))


def project_kv(scalars, x_own, x_other, w):
    rows, half = x_own.shape
    width = w.shape[1] // 3
    heads = width // HD
    return call(
        functools.partial(kv_kernel, heads),
        (2, 2),
        [
            whole((rows, half)),
            whole((rows, half)),
            pl.BlockSpec((half, width), lambda n, k, s: ((k + s[0]) % 2, n)),
        ],
        [
            pl.BlockSpec((rows, width), lambda n, k, s: (0, n)),
            pl.BlockSpec((96, width), lambda n, k, s: (0, n)),
        ],
        [
            jax.ShapeDtypeStruct((rows, 2 * width), BF16),
            jax.ShapeDtypeStruct((96, 2 * width), BF16),
        ],
        [pltpu.VMEM((rows, width), F32)],
        8 * rows * half * width,
        8 * half * width,
    )(scalars, x_own, x_other, w)


def attend_local(scalars, x_own, x_other, w, kv):
    rows, half = x_own.shape
    width = w.shape[1] // 3
    heads = width // HD
    return call(
        functools.partial(local_kernel, heads),
        (2,),
        [
            whole((rows, half)),
            whole((rows, half)),
            pl.BlockSpec((half, width), lambda k, s: ((k + s[0]) % 2, 2)),
            whole((rows, 2 * width)),
        ],
        [whole((rows, width)), whole((rows, width)), whole((rows, HD))],
        [
            jax.ShapeDtypeStruct((rows, width), BF16),
            jax.ShapeDtypeStruct((rows, width), F32),
            jax.ShapeDtypeStruct((rows, HD), F32),
        ],
        [pltpu.VMEM((rows, width), F32)],
        4 * rows * half * width,
        4 * half * width,
    )(scalars, x_own, x_other, w, kv)


def attend_remote(scalars, query, acc, stats, near, mid, far):
    rows, width = query.shape
    heads = width // HD
    return call(
        functools.partial(remote_kernel, heads),
        (1,),
        [
            whole(query.shape),
            whole(acc.shape),
            whole(stats.shape),
            whole(near.shape),
            whole(mid.shape),
            whole(far.shape),
        ],
        whole((rows, width)),
        jax.ShapeDtypeStruct((rows, width), BF16),
        [],
        4 * rows * 160 * width,
        rows * width * 8,
    )(scalars, query, acc, stats, near, mid, far)


def project_back(scalars, x_own, att_own, att_other, w):
    rows, half = x_own.shape
    width = att_own.shape[1]
    return call(
        back_kernel,
        (2,),
        [
            whole((rows, half)),
            whole((rows, width)),
            whole((rows, width)),
            pl.BlockSpec((width, half), lambda k, s: ((k + s[0]) % 2, 0)),
        ],
        whole((rows, half)),
        jax.ShapeDtypeStruct((rows, half), BF16),
        [pltpu.VMEM((rows, half), F32)],
        4 * rows * half * width,
        4 * half * width,
    )(scalars, x_own, att_own, att_other, w)


def swap(value):
    count = lax.axis_size("seq")
    return lax.ppermute(value, "seq", [(i, i ^ 1) for i in range(count)])


def to_later_chip(value, steps):
    count = lax.axis_size("seq")
    pairs = []
    for source in range(count):
        if (source // 2) % GROUP_CHIPS + steps < GROUP_CHIPS:
            pairs.append((source, source + 2 * steps))
    return lax.ppermute(value, "seq", pairs)


def in_order(core, own, other, axis):
    return jnp.where(
        core == 0,
        jnp.concatenate([own, other], axis=axis),
        jnp.concatenate([other, own], axis=axis),
    )


def gather_chips(block):
    count = lax.axis_size("seq")
    groups = [list(range(core, count, 2)) for core in range(2)]
    return lax.all_gather(block, "seq", axis=0, tiled=True, axis_index_groups=groups)


def local(tokens, w_qkv, w_out, offsets):
    section = lax.axis_index("section")
    section_count = lax.axis_size("section")
    seq = lax.axis_index("seq")
    core = seq % 2
    scalars = jnp.concatenate(
        [
            jnp.stack([core, (seq // 2) % GROUP_CHIPS]).astype(jnp.int32),
            offsets.reshape(-1).astype(jnp.int32),
        ]
    )
    with jax.named_scope("weights"):
        rows = w_qkv.shape[1]
        width = w_qkv.shape[2] // 6
        parts = w_qkv[0].reshape(rows, 3, 2, width)
        halves = [
            jnp.concatenate([parts[:, 1, h], parts[:, 2, h], parts[:, 0, h]], axis=1)
            for h in range(2)
        ]
        own = jnp.where(core == 0, halves[0], halves[1])
        other = swap(jnp.where(core == 0, halves[1], halves[0]))
        w_in = gather_chips(in_order(core, own, other, 0))
        cut = w_out.shape[2] // 2
        left, right = w_out[0][:, :cut], w_out[0][:, cut:]
        own = jnp.where(core == 0, left, right)
        other = swap(jnp.where(core == 0, right, left))
        w_back = gather_chips(in_order(core, own, other, 0))
    with jax.named_scope("tokens"):
        both = in_order(core, tokens[0], swap(tokens[0]), 0)
        left, right = both[:, :cut], both[:, cut:]
        x_own = jnp.where(core == 0, left, right)
        x_other = jnp.where(core == 0, right, left)
    result = jnp.zeros_like(x_own)
    for tick in range(section_count):
        kv, send = project_kv(scalars, x_own, x_other, w_in)
        near = to_later_chip(send, 1)
        mid = to_later_chip(send[64:], 2)
        far = to_later_chip(send[64:], 3)
        query, acc, stats = attend_local(scalars, x_own, x_other, w_in, kv)
        att = attend_remote(scalars, query, acc, stats, near, mid, far)
        produced = project_back(scalars, x_own, att, swap(att), w_back)
        result = jnp.where(section == tick, produced, result)
        if tick + 1 < section_count:
            x_own = lax.ppermute(produced, "section", [(tick, tick + 1)])
            x_other = swap(x_own)
    with jax.named_scope("result"):
        top, bottom = result[:128], result[128:]
        mine = jnp.where(core == 0, top, bottom)
        theirs = swap(jnp.where(core == 0, bottom, top))
        return in_order(core, mine, theirs, 1)[None, None]


def solution(mesh):
    return jax.shard_map(
        local,
        mesh=mesh,
        in_specs=(P(None, "seq", None), P("section", "seq", None), P("section", "seq", None), P()),
        out_specs=P("section", None, "seq", None),
        check_vma=False,
    )
```

```python
import functools
import math

import jax
import jax.numpy as jnp
from jax import lax
from jax.experimental import pallas as pl
from jax.experimental.pallas import tpu as pltpu
from jax.sharding import PartitionSpec as P

NEG_FILL = -1e30
HD = 128
CHIP_ROWS = 256
GROUP_CHIPS = 4
BF16 = jnp.bfloat16
F32 = jnp.float32
VMEM_LIMIT = 32 * 1024 * 1024


def dot(a, b):
    return lax.dot_general(a, b, (((1,), (0,)), ((), ())), preferred_element_type=F32)


def dot_t(a, b):
    return lax.dot_general(a, b, (((1,), (1,)), ((), ())), preferred_element_type=F32)


def offset_of(scalars, branch, head_at, heads):
    return scalars[2 + branch * 2 * heads + scalars[0] * heads + head_at]


def kv_kernel(heads, scalars, x_own, x_other, w, kv_out, send_out, acc):
    half = pl.program_id(1)

    @pl.when(half == 0)
    def _():
        acc[...] = dot(x_own[...], w[...])

    @pl.when(half == 1)
    def _():
        rows = (acc[...] + dot(x_other[...], w[...])).astype(BF16)
        kv_out[...] = rows
        row = lax.broadcasted_iota(jnp.int32, (96, CHIP_ROWS), 0)
        col = lax.broadcasted_iota(jnp.int32, (96, CHIP_ROWS), 1)
        for i in range(heads):
            off2 = offset_of(scalars, 2, i, heads)
            off3 = offset_of(scalars, 3, i, heads)
            source = jnp.where(row < 64, 4 * row + off2, 8 * (row - 64) + off3)
            pick = jnp.where(col == source, 1.0, 0.0).astype(BF16)
            cols = slice(i * HD, (i + 1) * HD)
            send_out[:, cols] = dot(pick, rows[:, cols]).astype(BF16)


def local_kernel(heads, scalars, x_own, x_other, w, kv, q_out, acc_out, stat_out, acc):
    half = pl.program_id(0)

    @pl.when(half == 0)
    def _():
        acc[...] = dot(x_own[...], w[...])

    @pl.when(half == 1)
    def _():
        query = (acc[...] + dot(x_other[...], w[...])).astype(BF16)
        q_out[...] = query
        scaling = 1.0 / math.sqrt(HD)
        shape = (CHIP_ROWS, CHIP_ROWS)
        causal = lax.broadcasted_iota(jnp.int32, shape, 1) <= lax.broadcasted_iota(
            jnp.int32, shape, 0
        )
        row = lax.broadcasted_iota(jnp.int32, (CHIP_ROWS, HD), 0)
        lane = lax.broadcasted_iota(jnp.int32, (CHIP_ROWS, HD), 1)
        first = ((lane == 0) & (row < 128)) | ((lane == 1) & (row >= 128))
        period = jnp.where(lane == 2, 1, jnp.where(lane == 3, 3, 7))
        in_branch = (lane >= 2) & (lane <= 4)
        stats = jnp.zeros((CHIP_ROWS, HD), F32)
        width = heads * HD
        for i in range(heads):
            cols = slice(i * HD, (i + 1) * HD)
            offset = jnp.where(
                lane == 2,
                offset_of(scalars, 1, i, heads),
                jnp.where(
                    lane == 3, offset_of(scalars, 2, i, heads), offset_of(scalars, 3, i, heads)
                ),
            )
            member = first | (in_branch & ((row & period) == offset))
            member = jnp.where(member, 1.0, 0.0).astype(BF16)
            times = jnp.where(causal, dot_t(member, member), 0.0)
            scores = dot_t(query[:, cols], kv[:, cols]) * scaling
            scores = jnp.where(times > 0.0, scores, NEG_FILL)
            peak = jnp.max(scores, axis=1, keepdims=True)
            expos = times * jnp.exp(scores - peak)
            total = jnp.sum(expos, axis=1, keepdims=True)
            acc_out[:, cols] = dot(
                expos.astype(BF16), kv[:, width + i * HD : width + (i + 1) * HD]
            )
            stats = jnp.where(lane == i, peak, jnp.where(lane == heads + i, total, stats))
        stat_out[...] = stats


def remote_kernel(heads, scalars, query, acc, stats, near, mid, far, out):
    scaling = 1.0 / math.sqrt(HD)
    chip = scalars[1]
    width = heads * HD
    keys = 160
    row = lax.broadcasted_iota(jnp.int32, (CHIP_ROWS, keys), 0)
    col = lax.broadcasted_iota(jnp.int32, (CHIP_ROWS, keys), 1)
    second = (col < 64) & ((chip & 1) == 1)
    third = (col >= 64) & (chip >= 1 + (col - 64) // 32)
    stat = stats[...]
    for i in range(heads):
        cols = slice(i * HD, (i + 1) * HD)
        vals = slice(width + i * HD, width + (i + 1) * HD)
        off2 = offset_of(scalars, 2, i, heads)
        off3 = offset_of(scalars, 3, i, heads)
        allowed = (second & ((row & 3) == off2)) | (third & ((row & 7) == off3))
        key_rows = jnp.concatenate([near[:, cols], mid[:, cols], far[:, cols]], axis=0)
        value_rows = jnp.concatenate([near[:, vals], mid[:, vals], far[:, vals]], axis=0)
        scores = dot_t(query[:, cols], key_rows) * scaling
        scores = jnp.where(allowed, scores, NEG_FILL)
        peak = stat[:, i : i + 1]
        total = stat[:, heads + i : heads + i + 1]
        new_peak = jnp.maximum(peak, jnp.max(scores, axis=1, keepdims=True))
        expos = jnp.exp(scores - new_peak)
        shrink = jnp.exp(peak - new_peak)
        total = total * shrink + jnp.sum(expos, axis=1, keepdims=True)
        mixed = acc[:, cols] * shrink + dot(expos.astype(BF16), value_rows)
        out[:, cols] = (mixed / total).astype(BF16)


def back_kernel(scalars, x_own, att_own, att_other, w, out, acc):
    half = pl.program_id(0)

    @pl.when(half == 0)
    def _():
        acc[...] = x_own[...].astype(F32) + dot(att_own[...], w[...])

    @pl.when(half == 1)
    def _():
        out[...] = (acc[...] + dot(att_other[...], w[...])).astype(BF16)


def call(body, grid, in_specs, out_specs, out_shape, scratch, flops, moved):
    return pl.pallas_call(
        body,
        grid_spec=pltpu.PrefetchScalarGridSpec(
            num_scalar_prefetch=1,
            grid=grid,
            in_specs=in_specs,
            out_specs=out_specs,
            scratch_shapes=scratch,
        ),
        out_shape=out_shape,
        compiler_params=pltpu.CompilerParams(vmem_limit_bytes=VMEM_LIMIT),
        cost_estimate=pl.CostEstimate(flops=flops, bytes_accessed=moved, transcendentals=0),
    )


def whole(shape):
    return pl.BlockSpec(shape, lambda *_: (0,) * len(shape))


def project_kv(scalars, x_own, x_other, w):
    rows, half = x_own.shape
    width = w.shape[1] // 4
    heads = width // HD
    return call(
        functools.partial(kv_kernel, heads),
        (2, 2),
        [
            whole((rows, half)),
            whole((rows, half)),
            pl.BlockSpec((half, width), lambda n, k, s: ((k + s[0]) % 2, 2 * n + s[0])),
        ],
        [
            pl.BlockSpec((rows, width), lambda n, k, s: (0, n)),
            pl.BlockSpec((96, width), lambda n, k, s: (0, n)),
        ],
        [
            jax.ShapeDtypeStruct((rows, 2 * width), BF16),
            jax.ShapeDtypeStruct((96, 2 * width), BF16),
        ],
        [pltpu.VMEM((rows, width), F32)],
        8 * rows * half * width,
        8 * half * width,
    )(scalars, x_own, x_other, w)


def attend_local(scalars, x_own, x_other, w, kv):
    rows, half = x_own.shape
    width = w.shape[1]
    heads = width // HD
    return call(
        functools.partial(local_kernel, heads),
        (2,),
        [
            whole((rows, half)),
            whole((rows, half)),
            pl.BlockSpec((half, width), lambda k, s: ((k + s[0]) % 2, 0)),
            whole((rows, 2 * width)),
        ],
        [whole((rows, width)), whole((rows, width)), whole((rows, HD))],
        [
            jax.ShapeDtypeStruct((rows, width), BF16),
            jax.ShapeDtypeStruct((rows, width), F32),
            jax.ShapeDtypeStruct((rows, HD), F32),
        ],
        [pltpu.VMEM((rows, width), F32)],
        4 * rows * half * width,
        4 * half * width,
    )(scalars, x_own, x_other, w, kv)


def attend_remote(scalars, query, acc, stats, near, mid, far):
    rows, width = query.shape
    heads = width // HD
    return call(
        functools.partial(remote_kernel, heads),
        (1,),
        [
            whole(query.shape),
            whole(acc.shape),
            whole(stats.shape),
            whole(near.shape),
            whole(mid.shape),
            whole(far.shape),
        ],
        whole((rows, width)),
        jax.ShapeDtypeStruct((rows, width), BF16),
        [],
        4 * rows * 160 * width,
        rows * width * 8,
    )(scalars, query, acc, stats, near, mid, far)


def project_back(scalars, x_own, att_own, att_other, w):
    rows, half = x_own.shape
    width = att_own.shape[1]
    return call(
        back_kernel,
        (2,),
        [
            whole((rows, half)),
            whole((rows, width)),
            whole((rows, width)),
            pl.BlockSpec((width, half), lambda k, s: ((k + s[0]) % 2, 0)),
        ],
        whole((rows, half)),
        jax.ShapeDtypeStruct((rows, half), BF16),
        [pltpu.VMEM((rows, half), F32)],
        4 * rows * half * width,
        4 * half * width,
    )(scalars, x_own, att_own, att_other, w)


def swap(value):
    count = lax.axis_size("seq")
    return lax.ppermute(value, "seq", [(i, i ^ 1) for i in range(count)])


def to_later_chip(value, steps):
    count = lax.axis_size("seq")
    pairs = []
    for source in range(count):
        if (source // 2) % GROUP_CHIPS + steps < GROUP_CHIPS:
            pairs.append((source, source + 2 * steps))
    return lax.ppermute(value, "seq", pairs)


def in_order(core, own, other, axis):
    return jnp.where(
        core == 0,
        jnp.concatenate([own, other], axis=axis),
        jnp.concatenate([other, own], axis=axis),
    )


def ring(value, stride, length, steps):
    count = lax.axis_size("seq")
    pairs = []
    for target in range(count):
        at = (target // stride) % length
        source = target + ((at + steps) % length - at) * stride
        pairs.append((source, target))
    return lax.ppermute(value, "seq", pairs)


def gather_ring(value, stride, length, at, axis):
    shape = value.shape[:axis] + (length,) + value.shape[axis:]
    full = jnp.zeros(shape, value.dtype)
    pieces = [value] + [ring(value, stride, length, step) for step in (1, 3, 2) if step < length]
    for step, piece in zip((0, 1, 3, 2), pieces):
        place = (at + step) % length
        full = lax.dynamic_update_slice_in_dim(full, jnp.expand_dims(piece, axis), place, axis)
    return full


def local(tokens, w_qkv, w_out, offsets):
    section = lax.axis_index("section")
    section_count = lax.axis_size("section")
    seq = lax.axis_index("seq")
    core = seq % 2
    scalars = jnp.concatenate(
        [
            jnp.stack([core, (seq // 2) % GROUP_CHIPS]).astype(jnp.int32),
            offsets.reshape(-1).astype(jnp.int32),
        ]
    )
    with jax.named_scope("weights"):
        third = w_qkv.shape[2] // 3
        width = third // 2
        cut = w_out.shape[2] // 2
        x_count = lax.axis_size("seq") // (2 * GROUP_CHIPS)
        chip_x, chip_z = seq // (2 * GROUP_CHIPS), (seq // 2) % GROUP_CHIPS
        w_kv = lax.all_gather(w_qkv[0][:, third:], "seq", axis=0, tiled=True)
        left, right = w_qkv[0][:, :width], w_qkv[0][:, width:third]
        own = jnp.where(core == 0, left, right)
        other = swap(jnp.where(core == 0, right, left))
        block = in_order(core, own, other, 0)
        stacked = gather_ring(block, 2, GROUP_CHIPS, chip_z, 0)
        stacked = gather_ring(stacked, 2 * GROUP_CHIPS, x_count, chip_x, 0)
        w_q = stacked.reshape(-1, width)
        left, right = w_out[0][:, :cut], w_out[0][:, cut:]
        own = jnp.where(core == 0, left, right)
        other = swap(jnp.where(core == 0, right, left))
        block = in_order(core, own, other, 0)
        stacked = gather_ring(block, 2 * GROUP_CHIPS, x_count, chip_x, 0)
        stacked = gather_ring(stacked, 2, GROUP_CHIPS, chip_z, 1)
        w_back = stacked.reshape(-1, cut)
    with jax.named_scope("tokens"):
        both = in_order(core, tokens[0], swap(tokens[0]), 0)
        left, right = both[:, :cut], both[:, cut:]
        x_own = jnp.where(core == 0, left, right)
        x_other = jnp.where(core == 0, right, left)
    result = jnp.zeros_like(x_own)
    for tick in range(section_count):
        kv, send = project_kv(scalars, x_own, x_other, w_kv)
        far = to_later_chip(send[64:], 3)
        mid = to_later_chip(send[64:], 2)
        near = to_later_chip(send, 1)
        query, acc, stats = attend_local(scalars, x_own, x_other, w_q, kv)
        att = attend_remote(scalars, query, acc, stats, near, mid, far)
        produced = project_back(scalars, x_own, att, swap(att), w_back)
        result = jnp.where(section == tick, produced, result)
        if tick + 1 < section_count:
            x_own = lax.ppermute(produced, "section", [(tick, tick + 1)])
            x_other = swap(x_own)
    with jax.named_scope("result"):
        top, bottom = result[:128], result[128:]
        mine = jnp.where(core == 0, top, bottom)
        theirs = swap(jnp.where(core == 0, bottom, top))
        return in_order(core, mine, theirs, 1)[None, None]


def solution(mesh):
    return jax.shard_map(
        local,
        mesh=mesh,
        in_specs=(P(None, "seq", None), P("section", "seq", None), P("section", "seq", None), P()),
        out_specs=P("section", None, "seq", None),
        check_vma=False,
    )
```

```python
import math

import jax
import jax.numpy as jnp
from jax import lax
from jax.experimental import pallas as pl
from jax.experimental.pallas import tpu as pltpu
from jax.sharding import PartitionSpec as P

NEG_FILL = -1e30
HD = 128
CHIP_ROWS = 256
GROUP_CHIPS = 4
BF16 = jnp.bfloat16
F32 = jnp.float32
VMEM_LIMIT = 24 * 1024 * 1024


def dot(a, b):
    return lax.dot_general(a, b, (((1,), (0,)), ((), ())), preferred_element_type=F32)


def dot_t(a, b):
    return lax.dot_general(a, b, (((1,), (1,)), ((), ())), preferred_element_type=F32)


def offset_of(scalars, branch, head_at, heads):
    return scalars[2 + branch * 2 * heads + scalars[0] * heads + head_at]


def spread(target, scalars, own, other):
    half = own.shape[1]
    core = scalars[0]
    target[:, pl.ds(pl.multiple_of(core * half, 128), half)] = own[...]
    target[:, pl.ds(pl.multiple_of((1 - core) * half, 128), half)] = other[...]


def kv_kernel(scalars, x_own, x_other, w, x_out, kv_out, send_out):
    width = kv_out.shape[1]
    heads = width // (2 * HD)
    spread(x_out, scalars, x_own, x_other)
    kv_out[...] = dot(x_out[...], w[...]).astype(BF16)
    row = lax.broadcasted_iota(jnp.int32, (96, CHIP_ROWS), 0)
    col = lax.broadcasted_iota(jnp.int32, (96, CHIP_ROWS), 1)
    for i in range(heads):
        off2 = offset_of(scalars, 2, i, heads)
        off3 = offset_of(scalars, 3, i, heads)
        source = jnp.where(row < 64, 4 * row + off2, 8 * (row - 64) + off3)
        pick = jnp.where(col == source, 1.0, 0.0).astype(BF16)
        cols = slice(2 * i * HD, 2 * (i + 1) * HD)
        send_out[:, cols] = dot(pick, kv_out[:, cols]).astype(BF16)


def local_kernel(scalars, x, w, kv, q_out, acc_out, stat_out):
    width = q_out.shape[1]
    heads = width // HD
    q_out[...] = dot(x[...], w[...]).astype(BF16)
    scaling = 1.0 / math.sqrt(HD)
    row = lax.broadcasted_iota(jnp.int32, (CHIP_ROWS, HD), 0)
    lane = lax.broadcasted_iota(jnp.int32, (CHIP_ROWS, HD), 1)
    first = ((lane == 0) & (row < 128)) | ((lane == 1) & (row >= 128))
    period = jnp.where(lane == 2, 1, jnp.where(lane == 3, 3, 7))
    in_branch = (lane >= 2) & (lane <= 4)
    phase = row & period
    causal = []
    for r in range(2):
        shape = (128, 128 * (r + 1))
        causal.append(
            lax.broadcasted_iota(jnp.int32, shape, 1)
            <= lax.broadcasted_iota(jnp.int32, shape, 0) + 128 * r
        )
    lane_half = lax.broadcasted_iota(jnp.int32, (128, HD), 1)
    stats = [jnp.zeros((128, HD), F32) for _ in range(2)]
    for i in range(heads):
        cols = slice(i * HD, (i + 1) * HD)
        keys = slice(2 * i * HD, (2 * i + 1) * HD)
        vals = slice((2 * i + 1) * HD, (2 * i + 2) * HD)
        offset = jnp.where(
            lane == 2,
            offset_of(scalars, 1, i, heads),
            jnp.where(
                lane == 3, offset_of(scalars, 2, i, heads), offset_of(scalars, 3, i, heads)
            ),
        )
        member = first | (in_branch & (phase == offset))
        member = jnp.where(member, 1.0, 0.0).astype(BF16)
        for r in range(2):
            rows = slice(128 * r, 128 * (r + 1))
            seen = slice(0, 128 * (r + 1))
            times = jnp.where(causal[r], dot_t(member[rows], member[seen]), 0.0)
            scores = dot_t(q_out[rows, cols], kv[seen, keys]) * scaling
            scores = jnp.where(times > 0.0, scores, NEG_FILL)
            peak = jnp.max(scores, axis=1, keepdims=True)
            expos = times * jnp.exp(scores - peak)
            total = jnp.sum(expos, axis=1, keepdims=True)
            acc_out[rows, cols] = dot(expos.astype(BF16), kv[seen, vals])
            stats[r] = jnp.where(
                lane_half == i, peak, jnp.where(lane_half == heads + i, total, stats[r])
            )
    stat_out[:128] = stats[0]
    stat_out[128:] = stats[1]


def remote_kernel(scalars, query, acc, stat, near, mid, far, out):
    heads = out.shape[1] // HD
    scaling = 1.0 / math.sqrt(HD)
    chip = scalars[1]
    shape = (CHIP_ROWS, 160)
    row = lax.broadcasted_iota(jnp.int32, shape, 0)
    col = lax.broadcasted_iota(jnp.int32, shape, 1)
    second = (col < 64) & ((chip & 1) == 1)
    third = (col >= 64) & (chip >= 1 + (col - 64) // 32)
    row2 = jnp.where(second, row & 3, -1)
    row3 = jnp.where(third, row & 7, -1)
    for i in range(heads):
        cols = slice(i * HD, (i + 1) * HD)
        keys = slice(2 * i * HD, (2 * i + 1) * HD)
        vals = slice((2 * i + 1) * HD, (2 * i + 2) * HD)
        off2 = offset_of(scalars, 2, i, heads)
        off3 = offset_of(scalars, 3, i, heads)
        allowed = (row2 == off2) | (row3 == off3)
        key_rows = jnp.concatenate([near[:, keys], mid[:, keys], far[:, keys]], axis=0)
        value_rows = jnp.concatenate([near[:, vals], mid[:, vals], far[:, vals]], axis=0)
        scores = dot_t(query[:, cols], key_rows) * scaling
        scores = jnp.where(allowed, scores, NEG_FILL)
        peak = stat[:, i : i + 1]
        total = stat[:, heads + i : heads + i + 1]
        new_peak = jnp.maximum(peak, jnp.max(scores, axis=1, keepdims=True))
        expos = jnp.exp(scores - new_peak)
        shrink = jnp.exp(peak - new_peak)
        total = total * shrink + jnp.sum(expos, axis=1, keepdims=True)
        mixed = acc[:, cols] * shrink + dot(expos.astype(BF16), value_rows)
        out[:, cols] = (mixed / total).astype(BF16)


def back_kernel(scalars, x_own, att_own, att_other, w, out, att):
    spread(att, scalars, att_own, att_other)
    out[...] = (x_own[...].astype(F32) + dot(att[...], w[...])).astype(BF16)


def unpack_kv_kernel(w, out, sems):
    parts = sems.shape[0]
    rows = out.shape[0] // parts
    copies = []
    for i in range(parts):
        at = pl.ds(i * rows, rows)
        copies.append(
            pltpu.make_async_copy(
                w.at[at, pl.ds(0, out.shape[1])], out.at[at, :], sems.at[i]
            )
        )
    for copy in copies:
        copy.start()
    for copy in copies:
        copy.wait()


def unpack_rest_kernel(w, query, back, query_sems, back_sems):
    width = query.shape[1]
    copies = []
    parts = query_sems.shape[0]
    rows = query.shape[0] // parts
    for i in range(parts):
        at = pl.ds(i * rows, rows)
        copies.append(
            pltpu.make_async_copy(
                w.at[at, pl.ds(2 * width, width)], query.at[at, :], query_sems.at[i]
            )
        )
    chips = back_sems.shape[0] // 2
    rows = back.shape[0] // chips
    for i in range(chips):
        for h in range(2):
            copies.append(
                pltpu.make_async_copy(
                    w.at[pl.ds((2 * i + h) * rows, rows), pl.ds(3 * width, width)],
                    back.at[pl.ds(i * rows, rows), pl.ds(h * width, width)],
                    back_sems.at[2 * i + h],
                )
            )
    for copy in copies:
        copy.start()
    for copy in copies:
        copy.wait()


def unpack(body, w, out_shape, sems):
    return pl.pallas_call(
        body,
        in_specs=[pl.BlockSpec(memory_space=pl.ANY)],
        out_specs=jax.tree.map(lambda _: pl.BlockSpec(memory_space=pltpu.VMEM), out_shape),
        out_shape=out_shape,
        scratch_shapes=[pltpu.SemaphoreType.DMA((count,)) for count in sems],
        compiler_params=pltpu.CompilerParams(vmem_limit_bytes=VMEM_LIMIT),
    )(w)


def call(body, out_shape, scratch, flops, scalars, *operands):
    in_specs = [pl.BlockSpec(memory_space=pltpu.SMEM)]
    in_specs += [pl.BlockSpec(memory_space=pltpu.VMEM) for _ in operands]
    out_specs = jax.tree.map(lambda _: pl.BlockSpec(memory_space=pltpu.VMEM), out_shape)
    return pl.pallas_call(
        body,
        in_specs=in_specs,
        out_specs=out_specs,
        out_shape=out_shape,
        scratch_shapes=scratch,
        compiler_params=pltpu.CompilerParams(vmem_limit_bytes=VMEM_LIMIT),
        cost_estimate=pl.CostEstimate(flops=flops, bytes_accessed=2**20, transcendentals=0),
    )(scalars, *operands)


def project_kv(scalars, x_own, x_other, w):
    rows, half = x_own.shape
    width = w.shape[1] // 2
    return call(
        kv_kernel,
        [
            jax.ShapeDtypeStruct((rows, 2 * half), BF16),
            jax.ShapeDtypeStruct((rows, 2 * width), BF16),
            jax.ShapeDtypeStruct((96, 2 * width), BF16),
        ],
        [],
        8 * rows * half * width,
        scalars,
        x_own,
        x_other,
        w,
    )


def attend_local(scalars, x, w, kv):
    rows = x.shape[0]
    width = w.shape[1]
    return call(
        local_kernel,
        [
            jax.ShapeDtypeStruct((rows, width), BF16),
            jax.ShapeDtypeStruct((rows, width), F32),
            jax.ShapeDtypeStruct((rows, HD), F32),
        ],
        [],
        4 * rows * x.shape[1] * width,
        scalars,
        x,
        w,
        kv,
    )


def attend_remote(scalars, query, acc, stats, near, mid, far):
    rows, width = query.shape
    return call(
        remote_kernel,
        jax.ShapeDtypeStruct((rows, width), BF16),
        [],
        4 * rows * 160 * width,
        scalars,
        query,
        acc,
        stats,
        near,
        mid,
        far,
    )


def project_back(scalars, x_own, att_own, att_other, w):
    rows, half = x_own.shape
    width = att_own.shape[1]
    return call(
        back_kernel,
        jax.ShapeDtypeStruct((rows, half), BF16),
        [pltpu.VMEM((rows, 2 * width), BF16)],
        4 * rows * half * width,
        scalars,
        x_own,
        att_own,
        att_other,
        w,
    )


def swap(value):
    count = lax.axis_size("seq")
    return lax.ppermute(value, "seq", [(i, i ^ 1) for i in range(count)])


def to_later_chip(value, steps):
    count = lax.axis_size("seq")
    pairs = []
    for source in range(count):
        if (source // 2) % GROUP_CHIPS + steps < GROUP_CHIPS:
            pairs.append((source, source + 2 * steps))
    return lax.ppermute(value, "seq", pairs)


def in_order(core, own, other, axis):
    return jnp.where(
        core == 0,
        jnp.concatenate([own, other], axis=axis),
        jnp.concatenate([other, own], axis=axis),
    )


def gather_chips(block):
    count = lax.axis_size("seq")
    groups = [list(range(core, count, 2)) for core in range(2)]
    return lax.all_gather(block, "seq", axis=0, tiled=True, axis_index_groups=groups)


def local(tokens, w_qkv, w_out, offsets):
    section = lax.axis_index("section")
    section_count = lax.axis_size("section")
    seq = lax.axis_index("seq")
    core = seq % 2
    scalars = jnp.concatenate(
        [
            jnp.stack([core, (seq // 2) % GROUP_CHIPS]).astype(jnp.int32),
            offsets.reshape(-1).astype(jnp.int32),
        ]
    )
    with jax.named_scope("weights"):
        rows = w_qkv.shape[1]
        width = w_qkv.shape[2] // 6
        heads = width // HD
        cut = w_out.shape[2] // 2
        parts = w_qkv[0].reshape(rows, 3, 2, heads, HD)

        def half_of(h):
            kv = jnp.stack([parts[:, 1, h], parts[:, 2, h]], axis=2).reshape(rows, 2 * width)
            query = parts[:, 0, h].reshape(rows, width)
            back = w_out[0][:, h * cut : (h + 1) * cut]
            back = jnp.concatenate([back[:, :width], back[:, width:]], axis=0)
            return jnp.concatenate([kv, query, back], axis=1)

        halves = [half_of(0), half_of(1)]
        own = jnp.where(core == 0, halves[0], halves[1])
        other = swap(jnp.where(core == 0, halves[1], halves[0]))
        block = in_order(core, own[:, : 3 * width], other[:, : 3 * width], 0)
        back = [
            in_order(core, own[at, 3 * width :], other[at, 3 * width :], 0)
            for at in (slice(0, rows // 2), slice(rows // 2, rows))
        ]
        block = jnp.concatenate([block, jnp.concatenate(back, axis=0)], axis=1)
        w_all = gather_chips(block)
        depth = w_all.shape[0]
        w_kv = unpack(
            unpack_kv_kernel, w_all, jax.ShapeDtypeStruct((depth, 2 * width), BF16), [8]
        )
        w_q, w_back = unpack(
            unpack_rest_kernel,
            w_all,
            [
                jax.ShapeDtypeStruct((depth, width), BF16),
                jax.ShapeDtypeStruct((depth // 2, cut), BF16),
            ],
            [8, depth // rows],
        )
    with jax.named_scope("tokens"):
        both = in_order(core, tokens[0], swap(tokens[0]), 0)
        left, right = both[:, :cut], both[:, cut:]
        x_own = jnp.where(core == 0, left, right)
        x_other = jnp.where(core == 0, right, left)
    result = jnp.zeros_like(x_own)
    for tick in range(section_count):
        x, kv, send = project_kv(scalars, x_own, x_other, w_kv)
        near = to_later_chip(send, 1)
        mid = to_later_chip(send[64:], 2)
        far = to_later_chip(send[64:], 3)
        query, acc, stats = attend_local(scalars, x, w_q, kv)
        att = attend_remote(scalars, query, acc, stats, near, mid, far)
        produced = project_back(scalars, x_own, att, swap(att), w_back)
        result = jnp.where(section == tick, produced, result)
        if tick + 1 < section_count:
            x_own = lax.ppermute(produced, "section", [(tick, tick + 1)])
            x_other = swap(x_own)
    with jax.named_scope("result"):
        top, bottom = result[:128], result[128:]
        mine = jnp.where(core == 0, top, bottom)
        theirs = swap(jnp.where(core == 0, bottom, top))
        return in_order(core, mine, theirs, 1)[None, None]


def solution(mesh):
    return jax.shard_map(
        local,
        mesh=mesh,
        in_specs=(P(None, "seq", None), P("section", "seq", None), P("section", "seq", None), P()),
        out_specs=P("section", None, "seq", None),
        check_vma=False,
    )
```

```python
import math

import jax
import jax.numpy as jnp
from jax import lax
from jax.experimental import pallas as pl
from jax.experimental.pallas import tpu as pltpu
from jax.sharding import PartitionSpec as P

NEG_FILL = -1e30
HD = 128
CHIP_ROWS = 256
GROUP_CHIPS = 4
BF16 = jnp.bfloat16
F32 = jnp.float32
VMEM_LIMIT = 20 * 1024 * 1024
UNPACK_LIMIT = 46 * 1024 * 1024


def dot(a, b):
    return lax.dot_general(a, b, (((1,), (0,)), ((), ())), preferred_element_type=F32)


def dot_t(a, b):
    return lax.dot_general(a, b, (((1,), (1,)), ((), ())), preferred_element_type=F32)


def offset_of(scalars, branch, head_at, heads):
    return scalars[2 + branch * 2 * heads + scalars[0] * heads + head_at]


def rows_of(core, w):
    half = w.shape[0] // 2
    return w[pl.ds(pl.multiple_of(core * half, 128), half), :]


def early_kernel(scalars, own, w, acc):
    acc[...] = dot(own[...], rows_of(scalars[0], w))


def kv_kernel(scalars, acc, other, w, kv_out, send_out):
    width = kv_out.shape[1]
    heads = width // (2 * HD)
    kv_out[...] = (acc[...] + dot(other[...], rows_of(1 - scalars[0], w))).astype(BF16)
    row = lax.broadcasted_iota(jnp.int32, (96, CHIP_ROWS), 0)
    col = lax.broadcasted_iota(jnp.int32, (96, CHIP_ROWS), 1)
    for i in range(heads):
        off2 = offset_of(scalars, 2, i, heads)
        off3 = offset_of(scalars, 3, i, heads)
        source = jnp.where(row < 64, 4 * row + off2, 8 * (row - 64) + off3)
        pick = jnp.where(col == source, 1.0, 0.0).astype(BF16)
        cols = slice(2 * i * HD, 2 * (i + 1) * HD)
        send_out[:, cols] = dot(pick, kv_out[:, cols]).astype(BF16)


def local_kernel(scalars, own, other, w, kv, q_out, acc_out, stat_out):
    width = q_out.shape[1]
    heads = width // HD
    core = scalars[0]
    query = dot(own[...], rows_of(core, w)) + dot(other[...], rows_of(1 - core, w))
    q_out[...] = query.astype(BF16)
    scaling = 1.0 / math.sqrt(HD)
    row = lax.broadcasted_iota(jnp.int32, (CHIP_ROWS, HD), 0)
    lane = lax.broadcasted_iota(jnp.int32, (CHIP_ROWS, HD), 1)
    first = ((lane == 0) & (row < 128)) | ((lane == 1) & (row >= 128))
    period = jnp.where(lane == 2, 1, jnp.where(lane == 3, 3, 7))
    phase = jnp.where((lane >= 2) & (lane <= 4), row & period, -1)
    phase = jnp.where(first, -2, phase)
    causal = []
    for r in range(2):
        shape = (128, 128 * (r + 1))
        causal.append(
            lax.broadcasted_iota(jnp.int32, shape, 1)
            <= lax.broadcasted_iota(jnp.int32, shape, 0) + 128 * r
        )
    lane_half = lax.broadcasted_iota(jnp.int32, (128, HD), 1)
    stats = [jnp.zeros((128, HD), F32) for _ in range(2)]
    work = [(i, r) for i in range(heads) for r in range(2)]
    members = []
    for i in range(heads):
        offset = jnp.where(
            lane == 2,
            offset_of(scalars, 1, i, heads),
            jnp.where(
                lane == 3, offset_of(scalars, 2, i, heads), offset_of(scalars, 3, i, heads)
            ),
        )
        member = (phase == offset) | (phase == -2)
        members.append(jnp.where(member, 1.0, 0.0).astype(BF16))
    times, scores, peaks, expos = {}, {}, {}, {}
    for i, r in work:
        rows = slice(128 * r, 128 * (r + 1))
        seen = slice(0, 128 * (r + 1))
        times[i, r] = jnp.where(causal[r], dot_t(members[i][rows], members[i][seen]), 0.0)
        keys = slice(2 * i * HD, (2 * i + 1) * HD)
        raw = dot_t(q_out[rows, i * HD : (i + 1) * HD], kv[seen, keys]) * scaling
        scores[i, r] = jnp.where(times[i, r] > 0.0, raw, NEG_FILL)
    for at in work:
        peaks[at] = jnp.max(scores[at], axis=1, keepdims=True)
    for at in work:
        expos[at] = times[at] * jnp.exp(scores[at] - peaks[at])
    for i, r in work:
        rows = slice(128 * r, 128 * (r + 1))
        seen = slice(0, 128 * (r + 1))
        vals = slice((2 * i + 1) * HD, (2 * i + 2) * HD)
        acc_out[rows, i * HD : (i + 1) * HD] = dot(expos[i, r].astype(BF16), kv[seen, vals])
    for i, r in work:
        total = jnp.sum(expos[i, r], axis=1, keepdims=True)
        stats[r] = jnp.where(
            lane_half == i, peaks[i, r], jnp.where(lane_half == heads + i, total, stats[r])
        )
    stat_out[:128] = stats[0]
    stat_out[128:] = stats[1]


def remote_kernel(scalars, query, acc, stat, near, mid, far, out):
    heads = out.shape[1] // HD
    scaling = 1.0 / math.sqrt(HD)
    chip = scalars[1]
    shape = (CHIP_ROWS, 160)
    row = lax.broadcasted_iota(jnp.int32, shape, 0)
    col = lax.broadcasted_iota(jnp.int32, shape, 1)
    second = (col < 64) & ((chip & 1) == 1)
    third = (col >= 64) & (chip >= 1 + (col - 64) // 32)
    row2 = jnp.where(second, row & 3, -1)
    row3 = jnp.where(third, row & 7, -1)
    scores, peaks, expos, mixed = [], [], [], []
    for i in range(heads):
        keys = slice(2 * i * HD, (2 * i + 1) * HD)
        off2 = offset_of(scalars, 2, i, heads)
        off3 = offset_of(scalars, 3, i, heads)
        allowed = (row2 == off2) | (row3 == off3)
        key_rows = jnp.concatenate([near[:, keys], mid[:, keys], far[:, keys]], axis=0)
        raw = dot_t(query[:, i * HD : (i + 1) * HD], key_rows) * scaling
        scores.append(jnp.where(allowed, raw, NEG_FILL))
    for i in range(heads):
        peaks.append(jnp.maximum(stat[:, i : i + 1], jnp.max(scores[i], axis=1, keepdims=True)))
    for i in range(heads):
        expos.append(jnp.exp(scores[i] - peaks[i]))
    for i in range(heads):
        vals = slice((2 * i + 1) * HD, (2 * i + 2) * HD)
        value_rows = jnp.concatenate([near[:, vals], mid[:, vals], far[:, vals]], axis=0)
        mixed.append(dot(expos[i].astype(BF16), value_rows))
    for i in range(heads):
        cols = slice(i * HD, (i + 1) * HD)
        shrink = jnp.exp(stat[:, i : i + 1] - peaks[i])
        total = stat[:, heads + i : heads + i + 1] * shrink
        total = total + jnp.sum(expos[i], axis=1, keepdims=True)
        inverse = 1.0 / total
        out[:, cols] = (acc[:, cols] * (shrink * inverse) + mixed[i] * inverse).astype(BF16)


def back_early_kernel(scalars, x_own, att_own, w, acc):
    acc[...] = x_own[...].astype(F32) + dot(att_own[...], rows_of(scalars[0], w))


def back_kernel(scalars, acc, att_other, w, out):
    out[...] = (acc[...] + dot(att_other[...], rows_of(1 - scalars[0], w))).astype(BF16)


def unpack_kv_kernel(w, out, sems):
    parts = sems.shape[0]
    rows = out.shape[0] // parts
    copies = []
    for i in range(parts):
        at = pl.ds(i * rows, rows)
        copies.append(
            pltpu.make_async_copy(
                w.at[at, pl.ds(0, out.shape[1])], out.at[at, :], sems.at[i]
            )
        )
    for copy in copies:
        copy.start()
    for copy in copies:
        copy.wait()


def unpack_rest_kernel(w, query, back, query_sems, back_sems):
    width = query.shape[1]
    copies = []
    parts = query_sems.shape[0]
    rows = query.shape[0] // parts
    for i in range(parts):
        at = pl.ds(i * rows, rows)
        copies.append(
            pltpu.make_async_copy(
                w.at[at, pl.ds(2 * width, width)], query.at[at, :], query_sems.at[i]
            )
        )
    chips = back_sems.shape[0] // 2
    rows = back.shape[0] // chips
    for i in range(chips):
        for h in range(2):
            copies.append(
                pltpu.make_async_copy(
                    w.at[pl.ds((2 * i + h) * rows, rows), pl.ds(3 * width, width)],
                    back.at[pl.ds(i * rows, rows), pl.ds(h * width, width)],
                    back_sems.at[2 * i + h],
                )
            )
    for copy in copies:
        copy.start()
    for copy in copies:
        copy.wait()


def unpack(body, w, out_shape, sems):
    return pl.pallas_call(
        body,
        in_specs=[pl.BlockSpec(memory_space=pl.ANY)],
        out_specs=jax.tree.map(lambda _: pl.BlockSpec(memory_space=pltpu.VMEM), out_shape),
        out_shape=out_shape,
        scratch_shapes=[pltpu.SemaphoreType.DMA((count,)) for count in sems],
        compiler_params=pltpu.CompilerParams(vmem_limit_bytes=UNPACK_LIMIT),
    )(w)


def call(body, out_shape, flops, scalars, *operands):
    in_specs = [pl.BlockSpec(memory_space=pltpu.SMEM)]
    in_specs += [pl.BlockSpec(memory_space=pltpu.VMEM) for _ in operands]
    out_specs = jax.tree.map(lambda _: pl.BlockSpec(memory_space=pltpu.VMEM), out_shape)
    return pl.pallas_call(
        body,
        in_specs=in_specs,
        out_specs=out_specs,
        out_shape=out_shape,
        compiler_params=pltpu.CompilerParams(vmem_limit_bytes=VMEM_LIMIT),
        cost_estimate=pl.CostEstimate(flops=flops, bytes_accessed=1, transcendentals=0),
    )(scalars, *operands)


def project_early(scalars, own, w):
    rows, size = own.shape
    return call(
        early_kernel,
        jax.ShapeDtypeStruct((rows, w.shape[1]), F32),
        2 * rows * size * w.shape[1],
        scalars,
        own,
        w,
    )


def project_kv(scalars, acc, other, w):
    rows, width = acc.shape
    return call(
        kv_kernel,
        [
            jax.ShapeDtypeStruct((rows, width), BF16),
            jax.ShapeDtypeStruct((96, width), BF16),
        ],
        2 * rows * other.shape[1] * width,
        scalars,
        acc,
        other,
        w,
    )


def attend_local(scalars, own, other, w, kv):
    rows = own.shape[0]
    width = w.shape[1]
    return call(
        local_kernel,
        [
            jax.ShapeDtypeStruct((rows, width), BF16),
            jax.ShapeDtypeStruct((rows, width), F32),
            jax.ShapeDtypeStruct((rows, HD), F32),
        ],
        4 * rows * (own.shape[1] + 2 * HD) * width,
        scalars,
        own,
        other,
        w,
        kv,
    )


def attend_remote(scalars, query, acc, stats, near, mid, far):
    rows, width = query.shape
    return call(
        remote_kernel,
        jax.ShapeDtypeStruct((rows, width), BF16),
        4 * rows * 160 * width,
        scalars,
        query,
        acc,
        stats,
        near,
        mid,
        far,
    )


def project_back_early(scalars, x_own, att_own, w):
    rows, size = x_own.shape
    return call(
        back_early_kernel,
        jax.ShapeDtypeStruct((rows, size), F32),
        2 * rows * size * att_own.shape[1],
        scalars,
        x_own,
        att_own,
        w,
    )


def project_back(scalars, acc, att_other, w):
    rows, size = acc.shape
    return call(
        back_kernel,
        jax.ShapeDtypeStruct((rows, size), BF16),
        2 * rows * size * att_other.shape[1],
        scalars,
        acc,
        att_other,
        w,
    )


def swap(value):
    count = lax.axis_size("seq")
    return lax.ppermute(value, "seq", [(i, i ^ 1) for i in range(count)])


def to_later_chip(value, steps):
    count = lax.axis_size("seq")
    pairs = []
    for source in range(count):
        if (source // 2) % GROUP_CHIPS + steps < GROUP_CHIPS:
            pairs.append((source, source + 2 * steps))
    return lax.ppermute(value, "seq", pairs)


def in_order(core, own, other, axis):
    return jnp.where(
        core == 0,
        jnp.concatenate([own, other], axis=axis),
        jnp.concatenate([other, own], axis=axis),
    )


def gather_chips(block):
    count = lax.axis_size("seq")
    groups = [list(range(core, count, 2)) for core in range(2)]
    return lax.all_gather(block, "seq", axis=0, tiled=True, axis_index_groups=groups)


def local(tokens, w_qkv, w_out, offsets):
    section = lax.axis_index("section")
    section_count = lax.axis_size("section")
    seq = lax.axis_index("seq")
    core = seq % 2
    scalars = jnp.concatenate(
        [
            jnp.stack([core, (seq // 2) % GROUP_CHIPS]).astype(jnp.int32),
            offsets.reshape(-1).astype(jnp.int32),
        ]
    )
    with jax.named_scope("weights"):
        rows = w_qkv.shape[1]
        width = w_qkv.shape[2] // 6
        heads = width // HD
        cut = w_out.shape[2] // 2
        parts = w_qkv[0].reshape(rows, 3, 2, heads, HD)

        def half_of(h):
            kv = jnp.stack([parts[:, 1, h], parts[:, 2, h]], axis=2).reshape(rows, 2 * width)
            query = parts[:, 0, h].reshape(rows, width)
            back = w_out[0][:, h * cut : (h + 1) * cut]
            back = jnp.concatenate([back[:, :width], back[:, width:]], axis=0)
            return jnp.concatenate([kv, query, back], axis=1)

        halves = [half_of(0), half_of(1)]
        own = jnp.where(core == 0, halves[0], halves[1])
        other = swap(jnp.where(core == 0, halves[1], halves[0]))
        block = in_order(core, own[:, : 3 * width], other[:, : 3 * width], 0)
        back = [
            in_order(core, own[at, 3 * width :], other[at, 3 * width :], 0)
            for at in (slice(0, rows // 2), slice(rows // 2, rows))
        ]
        block = jnp.concatenate([block, jnp.concatenate(back, axis=0)], axis=1)
        w_all = gather_chips(block)
        depth = w_all.shape[0]
        w_kv = unpack(
            unpack_kv_kernel, w_all, jax.ShapeDtypeStruct((depth, 2 * width), BF16), [8]
        )
        w_q, w_back = unpack(
            unpack_rest_kernel,
            w_all,
            [
                jax.ShapeDtypeStruct((depth, width), BF16),
                jax.ShapeDtypeStruct((depth // 2, cut), BF16),
            ],
            [8, depth // rows],
        )
    with jax.named_scope("tokens"):
        both = in_order(core, tokens[0], swap(tokens[0]), 0)
        left, right = both[:, :cut], both[:, cut:]
        x_own = jnp.where(core == 0, left, right)
        x_other = jnp.where(core == 0, right, left)
    result = jnp.zeros_like(x_own)
    for tick in range(section_count):
        acc = project_early(scalars, x_own, w_kv)
        kv, send = project_kv(scalars, acc, x_other, w_kv)
        near = to_later_chip(send, 1)
        mid = to_later_chip(send[64:], 2)
        far = to_later_chip(send[64:], 3)
        query, acc, stats = attend_local(scalars, x_own, x_other, w_q, kv)
        att = attend_remote(scalars, query, acc, stats, near, mid, far)
        acc = project_back_early(scalars, x_own, att, w_back)
        produced = project_back(scalars, acc, swap(att), w_back)
        result = jnp.where(section == tick, produced, result)
        if tick + 1 < section_count:
            x_own = lax.ppermute(produced, "section", [(tick, tick + 1)])
            x_other = swap(x_own)
    with jax.named_scope("result"):
        top, bottom = result[:128], result[128:]
        mine = jnp.where(core == 0, top, bottom)
        theirs = swap(jnp.where(core == 0, bottom, top))
        return in_order(core, mine, theirs, 1)[None, None]


def solution(mesh):
    return jax.shard_map(
        local,
        mesh=mesh,
        in_specs=(P(None, "seq", None), P("section", "seq", None), P("section", "seq", None), P()),
        out_specs=P("section", None, "seq", None),
        check_vma=False,
    )
```

```python
import math

import jax
import jax.numpy as jnp
from jax import lax
from jax.experimental import pallas as pl
from jax.experimental.pallas import tpu as pltpu
from jax.sharding import PartitionSpec as P

NEG_FILL = -1e30
HD = 128
CHIP_ROWS = 256
GROUP_CHIPS = 4
BF16 = jnp.bfloat16
F32 = jnp.float32
VMEM_LIMIT = 20 * 1024 * 1024
UNPACK_LIMIT = 46 * 1024 * 1024
PACK_LIMIT = 60 * 1024 * 1024


def dot(a, b):
    return lax.dot_general(a, b, (((1,), (0,)), ((), ())), preferred_element_type=F32)


def dot_t(a, b):
    return lax.dot_general(a, b, (((1,), (1,)), ((), ())), preferred_element_type=F32)


def offset_of(scalars, branch, head_at, heads):
    return scalars[2 + branch * 2 * heads + scalars[0] * heads + head_at]


def rows_of(core, w):
    half = w.shape[0] // 2
    return w[pl.ds(pl.multiple_of(core * half, 128), half), :]


def early_kernel(scalars, own, w, acc):
    acc[...] = dot(own[...], rows_of(scalars[0], w))


def kv_kernel(scalars, acc, other, w, kv_out, send_out):
    width = kv_out.shape[1]
    heads = width // (2 * HD)
    kv_out[...] = (acc[...] + dot(other[...], rows_of(1 - scalars[0], w))).astype(BF16)
    row = lax.broadcasted_iota(jnp.int32, (96, CHIP_ROWS), 0)
    col = lax.broadcasted_iota(jnp.int32, (96, CHIP_ROWS), 1)
    for i in range(heads):
        off2 = offset_of(scalars, 2, i, heads)
        off3 = offset_of(scalars, 3, i, heads)
        source = jnp.where(row < 64, 4 * row + off2, 8 * (row - 64) + off3)
        pick = jnp.where(col == source, 1.0, 0.0).astype(BF16)
        cols = slice(2 * i * HD, 2 * (i + 1) * HD)
        send_out[:, cols] = dot(pick, kv_out[:, cols]).astype(BF16)


def with_ones(values):
    return jnp.concatenate([values, jnp.ones_like(values)], axis=1)


def local_kernel(scalars, own, other, w, kv, q_out, acc_out, stat_out):
    width = q_out.shape[1]
    heads = width // HD
    core = scalars[0]
    query = dot(own[...], rows_of(core, w)) + dot(other[...], rows_of(1 - core, w))
    q_out[...] = query.astype(BF16)
    scaling = 1.0 / math.sqrt(HD)
    row = lax.broadcasted_iota(jnp.int32, (CHIP_ROWS, HD), 0)
    lane = lax.broadcasted_iota(jnp.int32, (CHIP_ROWS, HD), 1)
    first = ((lane == 0) & (row < 128)) | ((lane == 1) & (row >= 128))
    period = jnp.where(lane == 2, 1, jnp.where(lane == 3, 3, 7))
    phase = jnp.where((lane >= 2) & (lane <= 4), row & period, -1)
    phase = jnp.where(first, -2, phase)
    causal = []
    for r in range(2):
        shape = (128, 128 * (r + 1))
        causal.append(
            lax.broadcasted_iota(jnp.int32, shape, 1)
            <= lax.broadcasted_iota(jnp.int32, shape, 0) + 128 * r
        )
    lane_half = lax.broadcasted_iota(jnp.int32, (128, HD), 1)
    stats = [jnp.zeros((128, HD), F32) for _ in range(2)]
    work = [(i, r) for i in range(heads) for r in range(2)]
    members = []
    for i in range(heads):
        offset = jnp.where(
            lane == 2,
            offset_of(scalars, 1, i, heads),
            jnp.where(
                lane == 3, offset_of(scalars, 2, i, heads), offset_of(scalars, 3, i, heads)
            ),
        )
        member = (phase == offset) | (phase == -2)
        members.append(jnp.where(member, 1.0, 0.0).astype(BF16))
    times, scores, peaks, expos = {}, {}, {}, {}
    for i, r in work:
        rows = slice(128 * r, 128 * (r + 1))
        seen = slice(0, 128 * (r + 1))
        times[i, r] = jnp.where(causal[r], dot_t(members[i][rows], members[i][seen]), 0.0)
        keys = slice(2 * i * HD, (2 * i + 1) * HD)
        raw = dot_t(q_out[rows, i * HD : (i + 1) * HD], kv[seen, keys]) * scaling
        scores[i, r] = jnp.where(times[i, r] > 0.0, raw, NEG_FILL)
    for at in work:
        peaks[at] = jnp.max(scores[at], axis=1, keepdims=True)
    for at in work:
        expos[at] = times[at] * jnp.exp(scores[at] - peaks[at])
    for i, r in work:
        rows = slice(128 * r, 128 * (r + 1))
        seen = slice(0, 128 * (r + 1))
        vals = slice((2 * i + 1) * HD, (2 * i + 2) * HD)
        acc_out[rows, 2 * i * HD : 2 * (i + 1) * HD] = dot(
            expos[i, r].astype(BF16), with_ones(kv[seen, vals])
        )
        stats[r] = jnp.where(lane_half == i, peaks[i, r], stats[r])
    stat_out[:128] = stats[0]
    stat_out[128:] = stats[1]


def remote_kernel(scalars, query, acc, stat, near, mid, far, out):
    heads = out.shape[1] // HD
    scaling = 1.0 / math.sqrt(HD)
    chip = scalars[1]
    shape = (CHIP_ROWS, 160)
    row = lax.broadcasted_iota(jnp.int32, shape, 0)
    col = lax.broadcasted_iota(jnp.int32, shape, 1)
    second = (col < 64) & ((chip & 1) == 1)
    third = (col >= 64) & (chip >= 1 + (col - 64) // 32)
    row2 = jnp.where(second, row & 3, -1)
    row3 = jnp.where(third, row & 7, -1)
    scores, peaks, expos, mixed = [], [], [], []
    for i in range(heads):
        keys = slice(2 * i * HD, (2 * i + 1) * HD)
        off2 = offset_of(scalars, 2, i, heads)
        off3 = offset_of(scalars, 3, i, heads)
        allowed = (row2 == off2) | (row3 == off3)
        key_rows = jnp.concatenate([near[:, keys], mid[:, keys], far[:, keys]], axis=0)
        raw = dot_t(query[:, i * HD : (i + 1) * HD], key_rows) * scaling
        scores.append(jnp.where(allowed, raw, NEG_FILL))
    for i in range(heads):
        peaks.append(jnp.maximum(stat[:, i : i + 1], jnp.max(scores[i], axis=1, keepdims=True)))
    for i in range(heads):
        expos.append(jnp.exp(scores[i] - peaks[i]))
    for i in range(heads):
        vals = slice((2 * i + 1) * HD, (2 * i + 2) * HD)
        value_rows = jnp.concatenate([near[:, vals], mid[:, vals], far[:, vals]], axis=0)
        mixed.append(dot(expos[i].astype(BF16), with_ones(value_rows)))
    for i in range(heads):
        shrink = jnp.exp(stat[:, i : i + 1] - peaks[i])
        both = acc[:, 2 * i * HD : 2 * (i + 1) * HD] * shrink + mixed[i]
        out[:, i * HD : (i + 1) * HD] = (both[:, :HD] / both[:, HD:]).astype(BF16)


def back_early_kernel(scalars, x_own, att_own, w, acc):
    acc[...] = x_own[...].astype(F32) + dot(att_own[...], rows_of(scalars[0], w))


def back_kernel(scalars, acc, att_other, w, out):
    out[...] = (acc[...] + dot(att_other[...], rows_of(1 - scalars[0], w))).astype(BF16)


def pack_kernel(core_ref, w_qkv_hbm, w_out_hbm, own, other, w_qkv, w_out, sems):
    copies = [
        pltpu.make_async_copy(w_qkv_hbm, w_qkv, sems.at[0]),
        pltpu.make_async_copy(w_out_hbm, w_out, sems.at[1]),
    ]
    for copy in copies:
        copy.start()
    third = w_qkv.shape[2] // 3
    width = third // 2
    cut = w_out.shape[2] // 2

    def columns(ref, start, size):
        return ref[0, :, pl.ds(pl.multiple_of(start, 128), size)]

    targets = ((own, core_ref[0]), (other, 1 - core_ref[0]))
    copies[0].wait()
    for target, core in targets:
        for i in range(width // HD):
            start = third + core * width + i * HD
            target[:, 2 * i * HD : (2 * i + 1) * HD] = columns(w_qkv, start, HD)
            target[:, (2 * i + 1) * HD : (2 * i + 2) * HD] = columns(w_qkv, start + third, HD)
        target[:, 2 * width : 3 * width] = columns(w_qkv, core * width, width)
    copies[1].wait()
    for target, core in targets:
        left = columns(w_out, core * cut, width).astype(F32)
        right = columns(w_out, core * cut + width, width).astype(F32)
        target[:, 3 * width :] = jnp.concatenate([left, right], axis=0).astype(BF16)


def join_kernel(core_ref, own, other, block):
    rows = own.shape[0]
    wide = block.shape[1] * 3 // 4
    core = core_ref[0]
    block[pl.ds(pl.multiple_of(core * rows, 16), rows), :wide] = own[:, :wide]
    block[pl.ds(pl.multiple_of((1 - core) * rows, 16), rows), :wide] = other[:, :wide]
    mine, theirs = own[:, wide:].astype(F32), other[:, wide:].astype(F32)
    first = jnp.where(core == 0, mine, theirs)
    second = jnp.where(core == 0, theirs, mine)
    half = rows // 2
    parts = [first[:half], second[:half], first[half:], second[half:]]
    block[:, wide:] = jnp.concatenate(parts, axis=0).astype(BF16)


def unpack_kv_kernel(w, out, sems):
    parts = sems.shape[0]
    rows = out.shape[0] // parts
    copies = []
    for i in range(parts):
        at = pl.ds(i * rows, rows)
        copies.append(
            pltpu.make_async_copy(
                w.at[at, pl.ds(0, out.shape[1])], out.at[at, :], sems.at[i]
            )
        )
    for copy in copies:
        copy.start()
    for copy in copies:
        copy.wait()


def unpack_rest_kernel(w, query, back, query_sems, back_sems):
    width = query.shape[1]
    copies = []
    parts = query_sems.shape[0]
    rows = query.shape[0] // parts
    for i in range(parts):
        at = pl.ds(i * rows, rows)
        copies.append(
            pltpu.make_async_copy(
                w.at[at, pl.ds(2 * width, width)], query.at[at, :], query_sems.at[i]
            )
        )
    chips = back_sems.shape[0] // 2
    rows = back.shape[0] // chips
    for i in range(chips):
        for h in range(2):
            copies.append(
                pltpu.make_async_copy(
                    w.at[pl.ds((2 * i + h) * rows, rows), pl.ds(3 * width, width)],
                    back.at[pl.ds(i * rows, rows), pl.ds(h * width, width)],
                    back_sems.at[2 * i + h],
                )
            )
    for copy in copies:
        copy.start()
    for copy in copies:
        copy.wait()


def unpack(body, w, out_shape, sems):
    return pl.pallas_call(
        body,
        in_specs=[pl.BlockSpec(memory_space=pl.ANY)],
        out_specs=jax.tree.map(lambda _: pl.BlockSpec(memory_space=pltpu.VMEM), out_shape),
        out_shape=out_shape,
        scratch_shapes=[pltpu.SemaphoreType.DMA((count,)) for count in sems],
        compiler_params=pltpu.CompilerParams(vmem_limit_bytes=UNPACK_LIMIT),
    )(w)


def call(body, out_shape, flops, scalars, *operands):
    in_specs = [pl.BlockSpec(memory_space=pltpu.SMEM)]
    in_specs += [pl.BlockSpec(memory_space=pltpu.VMEM) for _ in operands]
    out_specs = jax.tree.map(lambda _: pl.BlockSpec(memory_space=pltpu.VMEM), out_shape)
    return pl.pallas_call(
        body,
        in_specs=in_specs,
        out_specs=out_specs,
        out_shape=out_shape,
        compiler_params=pltpu.CompilerParams(vmem_limit_bytes=VMEM_LIMIT),
        cost_estimate=pl.CostEstimate(flops=flops, bytes_accessed=1, transcendentals=0),
    )(scalars, *operands)


def pack_weights(core, w_qkv, w_out):
    shape = (w_qkv.shape[1], w_qkv.shape[2] * 2 // 3)
    return pl.pallas_call(
        pack_kernel,
        in_specs=[pl.BlockSpec(memory_space=pltpu.SMEM)]
        + [pl.BlockSpec(memory_space=pl.ANY)] * 2,
        out_specs=[pl.BlockSpec(memory_space=pltpu.VMEM)] * 2,
        out_shape=[jax.ShapeDtypeStruct(shape, BF16)] * 2,
        scratch_shapes=[
            pltpu.VMEM(w_qkv.shape, BF16),
            pltpu.VMEM(w_out.shape, BF16),
            pltpu.SemaphoreType.DMA((2,)),
        ],
        compiler_params=pltpu.CompilerParams(vmem_limit_bytes=PACK_LIMIT),
    )(core, w_qkv, w_out)


def join_weights(core, own, other):
    shape = (2 * own.shape[0], own.shape[1])
    return call(join_kernel, jax.ShapeDtypeStruct(shape, BF16), 1, core, own, other)


def project_early(scalars, own, w):
    rows, size = own.shape
    return call(
        early_kernel,
        jax.ShapeDtypeStruct((rows, w.shape[1]), F32),
        2 * rows * size * w.shape[1],
        scalars,
        own,
        w,
    )


def project_kv(scalars, acc, other, w):
    rows, width = acc.shape
    return call(
        kv_kernel,
        [
            jax.ShapeDtypeStruct((rows, width), BF16),
            jax.ShapeDtypeStruct((96, width), BF16),
        ],
        2 * rows * other.shape[1] * width,
        scalars,
        acc,
        other,
        w,
    )


def attend_local(scalars, own, other, w, kv):
    rows = own.shape[0]
    width = w.shape[1]
    return call(
        local_kernel,
        [
            jax.ShapeDtypeStruct((rows, width), BF16),
            jax.ShapeDtypeStruct((rows, 2 * width), F32),
            jax.ShapeDtypeStruct((rows, HD), F32),
        ],
        4 * rows * (own.shape[1] + 2 * HD) * width,
        scalars,
        own,
        other,
        w,
        kv,
    )


def attend_remote(scalars, query, acc, stats, near, mid, far):
    rows, width = query.shape
    return call(
        remote_kernel,
        jax.ShapeDtypeStruct((rows, width), BF16),
        4 * rows * 160 * width,
        scalars,
        query,
        acc,
        stats,
        near,
        mid,
        far,
    )


def project_back_early(scalars, x_own, att_own, w):
    rows, size = x_own.shape
    return call(
        back_early_kernel,
        jax.ShapeDtypeStruct((rows, size), F32),
        2 * rows * size * att_own.shape[1],
        scalars,
        x_own,
        att_own,
        w,
    )


def project_back(scalars, acc, att_other, w):
    rows, size = acc.shape
    return call(
        back_kernel,
        jax.ShapeDtypeStruct((rows, size), BF16),
        2 * rows * size * att_other.shape[1],
        scalars,
        acc,
        att_other,
        w,
    )


def swap(value):
    count = lax.axis_size("seq")
    return lax.ppermute(value, "seq", [(i, i ^ 1) for i in range(count)])


def to_later_chip(value, steps):
    count = lax.axis_size("seq")
    pairs = []
    for source in range(count):
        if (source // 2) % GROUP_CHIPS + steps < GROUP_CHIPS:
            pairs.append((source, source + 2 * steps))
    return lax.ppermute(value, "seq", pairs)


def in_order(core, own, other, axis):
    return jnp.where(
        core == 0,
        jnp.concatenate([own, other], axis=axis),
        jnp.concatenate([other, own], axis=axis),
    )


def gather_chips(block):
    count = lax.axis_size("seq")
    groups = [list(range(core, count, 2)) for core in range(2)]
    return lax.all_gather(block, "seq", axis=0, tiled=True, axis_index_groups=groups)


def local(tokens, w_qkv, w_out, offsets):
    section = lax.axis_index("section")
    section_count = lax.axis_size("section")
    seq = lax.axis_index("seq")
    core = seq % 2
    scalars = jnp.concatenate(
        [
            jnp.stack([core, (seq // 2) % GROUP_CHIPS]).astype(jnp.int32),
            offsets.reshape(-1).astype(jnp.int32),
        ]
    )
    with jax.named_scope("weights"):
        rows = w_qkv.shape[1]
        width = w_qkv.shape[2] // 6
        cut = w_out.shape[2] // 2
        core_array = jnp.full((1,), core, jnp.int32)
        own, other = pack_weights(core_array, w_qkv, w_out)
        w_all = gather_chips(join_weights(core_array, own, swap(other)))
        depth = w_all.shape[0]
        w_kv = unpack(
            unpack_kv_kernel, w_all, jax.ShapeDtypeStruct((depth, 2 * width), BF16), [8]
        )
        w_q, w_back = unpack(
            unpack_rest_kernel,
            w_all,
            [
                jax.ShapeDtypeStruct((depth, width), BF16),
                jax.ShapeDtypeStruct((depth // 2, cut), BF16),
            ],
            [8, depth // rows],
        )
    with jax.named_scope("tokens"):
        both = in_order(core, tokens[0], swap(tokens[0]), 0)
        left, right = both[:, :cut], both[:, cut:]
        x_own = jnp.where(core == 0, left, right)
        x_other = jnp.where(core == 0, right, left)
    result = jnp.zeros_like(x_own)
    for tick in range(section_count):
        acc = project_early(scalars, x_own, w_kv)
        kv, send = project_kv(scalars, acc, x_other, w_kv)
        near = to_later_chip(send, 1)
        mid = to_later_chip(send[64:], 2)
        far = to_later_chip(send[64:], 3)
        query, acc, stats = attend_local(scalars, x_own, x_other, w_q, kv)
        att = attend_remote(scalars, query, acc, stats, near, mid, far)
        acc = project_back_early(scalars, x_own, att, w_back)
        produced = project_back(scalars, acc, swap(att), w_back)
        result = jnp.where(section == tick, produced, result)
        if tick + 1 < section_count:
            x_own = lax.ppermute(produced, "section", [(tick, tick + 1)])
            x_other = swap(x_own)
    with jax.named_scope("result"):
        top, bottom = result[:128], result[128:]
        mine = jnp.where(core == 0, top, bottom)
        theirs = swap(jnp.where(core == 0, bottom, top))
        return in_order(core, mine, theirs, 1)[None, None]


def solution(mesh):
    return jax.shard_map(
        local,
        mesh=mesh,
        in_specs=(P(None, "seq", None), P("section", "seq", None), P("section", "seq", None), P()),
        out_specs=P("section", None, "seq", None),
        check_vma=False,
    )
```

```python
import functools
import math

import jax
import jax.numpy as jnp
from jax import lax
from jax.experimental import pallas as pl
from jax.experimental.pallas import tpu as pltpu
from jax.sharding import PartitionSpec as P

NEG_FILL = -1e30
HD = 128
CHIP_ROWS = 256
GROUP_CHIPS = 4
BF16 = jnp.bfloat16
F32 = jnp.float32
VMEM_LIMIT = 20 * 1024 * 1024
UNPACK_LIMIT = 46 * 1024 * 1024
PACK_LIMIT = 60 * 1024 * 1024


def dot(a, b):
    return lax.dot_general(a, b, (((1,), (0,)), ((), ())), preferred_element_type=F32)


def dot_t(a, b):
    return lax.dot_general(a, b, (((1,), (1,)), ((), ())), preferred_element_type=F32)


def offset_of(scalars, branch, head_at, heads):
    return scalars[2 + branch * 2 * heads + scalars[0] * heads + head_at]


def rows_of(core, w):
    half = w.shape[0] // 2
    return w[pl.ds(pl.multiple_of(core * half, 128), half), :]


def early_kernel(scalars, own, w, acc):
    acc[...] = dot(own[...], rows_of(scalars[0], w))


def kv_kernel(scalars, acc, other, w, kv_out, pair_out, send_out):
    width = kv_out.shape[1]
    heads = width // (2 * HD)
    kv_out[...] = (acc[...] + dot(other[...], rows_of(1 - scalars[0], w))).astype(BF16)
    row = lax.broadcasted_iota(jnp.int32, (96, CHIP_ROWS), 0)
    col = lax.broadcasted_iota(jnp.int32, (96, CHIP_ROWS), 1)
    for i in range(heads):
        off2 = offset_of(scalars, 2, i, heads)
        off3 = offset_of(scalars, 3, i, heads)
        source = jnp.where(row < 64, 4 * row + off2, 8 * (row - 64) + off3)
        pick = jnp.where(col == source, 1.0, 0.0).astype(BF16)
        cols = slice(2 * i * HD, 2 * (i + 1) * HD)
        picked = dot(pick, kv_out[:, cols]).astype(BF16)
        pair_out[:, cols] = picked[:64]
        send_out[:, cols] = picked[64:]


def with_ones(values):
    return jnp.concatenate([values, jnp.ones_like(values)], axis=1)


def local_kernel(scalars, own, other, w, kv, q_out, acc_out, stat_out):
    width = q_out.shape[1]
    heads = width // HD
    core = scalars[0]
    query = dot(own[...], rows_of(core, w)) + dot(other[...], rows_of(1 - core, w))
    q_out[...] = query.astype(BF16)
    scaling = 1.0 / math.sqrt(HD)
    row = lax.broadcasted_iota(jnp.int32, (CHIP_ROWS, HD), 0)
    lane = lax.broadcasted_iota(jnp.int32, (CHIP_ROWS, HD), 1)
    first = ((lane == 0) & (row < 128)) | ((lane == 1) & (row >= 128))
    period = jnp.where(lane == 2, 1, jnp.where(lane == 3, 3, 7))
    phase = jnp.where((lane >= 2) & (lane <= 4), row & period, -1)
    phase = jnp.where(first, -2, phase)
    causal = []
    for r in range(2):
        shape = (128, 128 * (r + 1))
        causal.append(
            lax.broadcasted_iota(jnp.int32, shape, 1)
            <= lax.broadcasted_iota(jnp.int32, shape, 0) + 128 * r
        )
    lane_half = lax.broadcasted_iota(jnp.int32, (128, HD), 1)
    stats = [jnp.zeros((128, HD), F32) for _ in range(2)]
    work = [(i, r) for i in range(heads) for r in range(2)]
    members = []
    for i in range(heads):
        offset = jnp.where(
            lane == 2,
            offset_of(scalars, 1, i, heads),
            jnp.where(
                lane == 3, offset_of(scalars, 2, i, heads), offset_of(scalars, 3, i, heads)
            ),
        )
        member = (phase == offset) | (phase == -2)
        members.append(jnp.where(member, 1.0, 0.0).astype(BF16))
    times, scores, peaks, expos = {}, {}, {}, {}
    for i, r in work:
        rows = slice(128 * r, 128 * (r + 1))
        seen = slice(0, 128 * (r + 1))
        times[i, r] = jnp.where(causal[r], dot_t(members[i][rows], members[i][seen]), 0.0)
        keys = slice(2 * i * HD, (2 * i + 1) * HD)
        raw = dot_t(q_out[rows, i * HD : (i + 1) * HD], kv[seen, keys]) * scaling
        scores[i, r] = jnp.where(times[i, r] > 0.0, raw, NEG_FILL)
    for at in work:
        peaks[at] = jnp.max(scores[at], axis=1, keepdims=True)
    for at in work:
        expos[at] = times[at] * jnp.exp(scores[at] - peaks[at])
    for i, r in work:
        rows = slice(128 * r, 128 * (r + 1))
        seen = slice(0, 128 * (r + 1))
        vals = slice((2 * i + 1) * HD, (2 * i + 2) * HD)
        acc_out[rows, 2 * i * HD : 2 * (i + 1) * HD] = dot(
            expos[i, r].astype(BF16), with_ones(kv[seen, vals])
        )
        stats[r] = jnp.where(lane_half == i, peaks[i, r], stats[r])
    stat_out[:128] = stats[0]
    stat_out[128:] = stats[1]


def remote_kernel(scalars, query, acc, stat, pair, near, mid, far, out):
    heads = out.shape[1] // HD
    scaling = 1.0 / math.sqrt(HD)
    chip = scalars[1]
    shape = (CHIP_ROWS, 160)
    row = lax.broadcasted_iota(jnp.int32, shape, 0)
    col = lax.broadcasted_iota(jnp.int32, shape, 1)
    second = (col < 64) & ((chip & 1) == 1)
    third = (col >= 64) & (chip >= 1 + (col - 64) // 32)
    row2 = jnp.where(second, row & 3, -1)
    row3 = jnp.where(third, row & 7, -1)
    scores, peaks, expos, mixed = [], [], [], []
    for i in range(heads):
        keys = slice(2 * i * HD, (2 * i + 1) * HD)
        off2 = offset_of(scalars, 2, i, heads)
        off3 = offset_of(scalars, 3, i, heads)
        allowed = (row2 == off2) | (row3 == off3)
        key_rows = jnp.concatenate(
            [pair[:, keys], near[:, keys], mid[:, keys], far[:, keys]], axis=0
        )
        raw = dot_t(query[:, i * HD : (i + 1) * HD], key_rows) * scaling
        scores.append(jnp.where(allowed, raw, NEG_FILL))
    for i in range(heads):
        peaks.append(jnp.maximum(stat[:, i : i + 1], jnp.max(scores[i], axis=1, keepdims=True)))
    for i in range(heads):
        expos.append(jnp.exp(scores[i] - peaks[i]))
    for i in range(heads):
        vals = slice((2 * i + 1) * HD, (2 * i + 2) * HD)
        value_rows = jnp.concatenate(
            [pair[:, vals], near[:, vals], mid[:, vals], far[:, vals]], axis=0
        )
        mixed.append(dot(expos[i].astype(BF16), with_ones(value_rows)))
    for i in range(heads):
        shrink = jnp.exp(stat[:, i : i + 1] - peaks[i])
        both = acc[:, 2 * i * HD : 2 * (i + 1) * HD] * shrink + mixed[i]
        out[:, i * HD : (i + 1) * HD] = (both[:, :HD] / both[:, HD:]).astype(BF16)


def back_early_kernel(scalars, x_own, att_own, w, acc):
    acc[...] = x_own[...].astype(F32) + dot(att_own[...], rows_of(scalars[0], w))


def back_kernel(tick, scalars, acc, att_other, w, earlier, out, result):
    out[...] = (acc[...] + dot(att_other[...], rows_of(1 - scalars[0], w))).astype(BF16)
    mine = scalars[scalars.shape[0] - 1] == tick

    @pl.when(mine)
    def _():
        result[...] = out[...]

    @pl.when(jnp.logical_not(mine))
    def _():
        result[...] = earlier[...]


def pack_kernel(core_ref, w_qkv_hbm, w_out_hbm, own, other, w_qkv, w_out, sems):
    copies = [
        pltpu.make_async_copy(w_qkv_hbm, w_qkv, sems.at[0]),
        pltpu.make_async_copy(w_out_hbm, w_out, sems.at[1]),
    ]
    for copy in copies:
        copy.start()
    third = w_qkv.shape[2] // 3
    width = third // 2
    cut = w_out.shape[2] // 2

    def columns(ref, start, size):
        return ref[0, :, pl.ds(pl.multiple_of(start, 128), size)]

    targets = ((own, core_ref[0]), (other, 1 - core_ref[0]))
    copies[0].wait()
    for target, core in targets:
        for i in range(width // HD):
            start = third + core * width + i * HD
            target[:, 2 * i * HD : (2 * i + 1) * HD] = columns(w_qkv, start, HD)
            target[:, (2 * i + 1) * HD : (2 * i + 2) * HD] = columns(w_qkv, start + third, HD)
        target[:, 2 * width : 3 * width] = columns(w_qkv, core * width, width)
    copies[1].wait()
    for target, core in targets:
        left = columns(w_out, core * cut, width).astype(F32)
        right = columns(w_out, core * cut + width, width).astype(F32)
        target[:, 3 * width :] = jnp.concatenate([left, right], axis=0).astype(BF16)


def join_kernel(core_ref, own, other, block):
    rows = own.shape[0]
    wide = block.shape[1] * 3 // 4
    core = core_ref[0]
    block[pl.ds(pl.multiple_of(core * rows, 16), rows), :wide] = own[:, :wide]
    block[pl.ds(pl.multiple_of((1 - core) * rows, 16), rows), :wide] = other[:, :wide]
    mine, theirs = own[:, wide:].astype(F32), other[:, wide:].astype(F32)
    first = jnp.where(core == 0, mine, theirs)
    second = jnp.where(core == 0, theirs, mine)
    half = rows // 2
    parts = [first[:half], second[:half], first[half:], second[half:]]
    block[:, wide:] = jnp.concatenate(parts, axis=0).astype(BF16)


def unpack_kv_kernel(w, out, sems):
    parts = sems.shape[0]
    rows = out.shape[0] // parts
    copies = []
    for i in range(parts):
        at = pl.ds(i * rows, rows)
        copies.append(
            pltpu.make_async_copy(
                w.at[at, pl.ds(0, out.shape[1])], out.at[at, :], sems.at[i]
            )
        )
    for copy in copies:
        copy.start()
    for copy in copies:
        copy.wait()


def unpack_rest_kernel(w, query, back, query_sems, back_sems):
    width = query.shape[1]
    copies = []
    parts = query_sems.shape[0]
    rows = query.shape[0] // parts
    for i in range(parts):
        at = pl.ds(i * rows, rows)
        copies.append(
            pltpu.make_async_copy(
                w.at[at, pl.ds(2 * width, width)], query.at[at, :], query_sems.at[i]
            )
        )
    chips = back_sems.shape[0] // 2
    rows = back.shape[0] // chips
    for i in range(chips):
        for h in range(2):
            copies.append(
                pltpu.make_async_copy(
                    w.at[pl.ds((2 * i + h) * rows, rows), pl.ds(3 * width, width)],
                    back.at[pl.ds(i * rows, rows), pl.ds(h * width, width)],
                    back_sems.at[2 * i + h],
                )
            )
    for copy in copies:
        copy.start()
    for copy in copies:
        copy.wait()


def unpack(body, w, out_shape, sems):
    return pl.pallas_call(
        body,
        in_specs=[pl.BlockSpec(memory_space=pl.ANY)],
        out_specs=jax.tree.map(lambda _: pl.BlockSpec(memory_space=pltpu.VMEM), out_shape),
        out_shape=out_shape,
        scratch_shapes=[pltpu.SemaphoreType.DMA((count,)) for count in sems],
        compiler_params=pltpu.CompilerParams(vmem_limit_bytes=UNPACK_LIMIT),
    )(w)


def call(body, out_shape, flops, scalars, *operands):
    in_specs = [pl.BlockSpec(memory_space=pltpu.SMEM)]
    in_specs += [pl.BlockSpec(memory_space=pltpu.VMEM) for _ in operands]
    out_specs = jax.tree.map(lambda _: pl.BlockSpec(memory_space=pltpu.VMEM), out_shape)
    return pl.pallas_call(
        body,
        in_specs=in_specs,
        out_specs=out_specs,
        out_shape=out_shape,
        compiler_params=pltpu.CompilerParams(vmem_limit_bytes=VMEM_LIMIT),
        cost_estimate=pl.CostEstimate(flops=flops, bytes_accessed=1, transcendentals=0),
    )(scalars, *operands)


def pack_weights(core, w_qkv, w_out):
    shape = (w_qkv.shape[1], w_qkv.shape[2] * 2 // 3)
    return pl.pallas_call(
        pack_kernel,
        in_specs=[pl.BlockSpec(memory_space=pltpu.SMEM)]
        + [pl.BlockSpec(memory_space=pl.ANY)] * 2,
        out_specs=[pl.BlockSpec(memory_space=pltpu.VMEM)] * 2,
        out_shape=[jax.ShapeDtypeStruct(shape, BF16)] * 2,
        scratch_shapes=[
            pltpu.VMEM(w_qkv.shape, BF16),
            pltpu.VMEM(w_out.shape, BF16),
            pltpu.SemaphoreType.DMA((2,)),
        ],
        compiler_params=pltpu.CompilerParams(vmem_limit_bytes=PACK_LIMIT),
    )(core, w_qkv, w_out)


def join_weights(core, own, other):
    shape = (2 * own.shape[0], own.shape[1])
    return call(join_kernel, jax.ShapeDtypeStruct(shape, BF16), 1, core, own, other)


def project_early(scalars, own, w):
    rows, size = own.shape
    return call(
        early_kernel,
        jax.ShapeDtypeStruct((rows, w.shape[1]), F32),
        2 * rows * size * w.shape[1],
        scalars,
        own,
        w,
    )


def project_kv(scalars, acc, other, w):
    rows, width = acc.shape
    return call(
        kv_kernel,
        [
            jax.ShapeDtypeStruct((rows, width), BF16),
            jax.ShapeDtypeStruct((64, width), BF16),
            jax.ShapeDtypeStruct((32, width), BF16),
        ],
        2 * rows * other.shape[1] * width,
        scalars,
        acc,
        other,
        w,
    )


def attend_local(scalars, own, other, w, kv):
    rows = own.shape[0]
    width = w.shape[1]
    return call(
        local_kernel,
        [
            jax.ShapeDtypeStruct((rows, width), BF16),
            jax.ShapeDtypeStruct((rows, 2 * width), F32),
            jax.ShapeDtypeStruct((rows, HD), F32),
        ],
        4 * rows * (own.shape[1] + 2 * HD) * width,
        scalars,
        own,
        other,
        w,
        kv,
    )


def attend_remote(scalars, query, acc, stats, *sent):
    rows, width = query.shape
    return call(
        remote_kernel,
        jax.ShapeDtypeStruct((rows, width), BF16),
        4 * rows * 160 * width,
        scalars,
        query,
        acc,
        stats,
        *sent,
    )


def project_back_early(scalars, x_own, att_own, w):
    rows, size = x_own.shape
    return call(
        back_early_kernel,
        jax.ShapeDtypeStruct((rows, size), F32),
        2 * rows * size * att_own.shape[1],
        scalars,
        x_own,
        att_own,
        w,
    )


def project_back(scalars, tick, acc, att_other, w, earlier):
    rows, size = acc.shape
    return call(
        functools.partial(back_kernel, tick),
        [jax.ShapeDtypeStruct((rows, size), BF16)] * 2,
        2 * rows * size * att_other.shape[1],
        scalars,
        acc,
        att_other,
        w,
        earlier,
    )


def swap(value):
    count = lax.axis_size("seq")
    return lax.ppermute(value, "seq", [(i, i ^ 1) for i in range(count)])


def to_later_chip(value, steps):
    count = lax.axis_size("seq")
    pairs = []
    for source in range(count):
        if (source // 2) % GROUP_CHIPS + steps < GROUP_CHIPS:
            pairs.append((source, source + 2 * steps))
    return lax.ppermute(value, "seq", pairs)


def to_partner_chip(value):
    count = lax.axis_size("seq")
    pairs = [(source, source + 2) for source in range(count) if (source // 2) % 2 == 0]
    return lax.ppermute(value, "seq", pairs)


def in_order(core, own, other, axis):
    return jnp.where(
        core == 0,
        jnp.concatenate([own, other], axis=axis),
        jnp.concatenate([other, own], axis=axis),
    )


def gather_chips(block):
    count = lax.axis_size("seq")
    groups = [list(range(core, count, 2)) for core in range(2)]
    return lax.all_gather(block, "seq", axis=0, tiled=True, axis_index_groups=groups)


def local(tokens, w_qkv, w_out, offsets):
    section = lax.axis_index("section")
    section_count = lax.axis_size("section")
    seq = lax.axis_index("seq")
    core = seq % 2
    scalars = jnp.concatenate(
        [
            jnp.stack([core, (seq // 2) % GROUP_CHIPS]).astype(jnp.int32),
            offsets.reshape(-1).astype(jnp.int32),
            jnp.full((1,), section, jnp.int32),
        ]
    )
    with jax.named_scope("weights"):
        rows = w_qkv.shape[1]
        width = w_qkv.shape[2] // 6
        cut = w_out.shape[2] // 2
        core_array = jnp.full((1,), core, jnp.int32)
        own, other = pack_weights(core_array, w_qkv, w_out)
        block = join_weights(core_array, own, swap(other))
        block, tokens = lax.optimization_barrier((block, tokens))
        w_all = gather_chips(block)
        depth = w_all.shape[0]
        w_kv = unpack(
            unpack_kv_kernel, w_all, jax.ShapeDtypeStruct((depth, 2 * width), BF16), [8]
        )
        w_q, w_back = unpack(
            unpack_rest_kernel,
            w_all,
            [
                jax.ShapeDtypeStruct((depth, width), BF16),
                jax.ShapeDtypeStruct((depth // 2, cut), BF16),
            ],
            [8, depth // rows],
        )
    with jax.named_scope("tokens"):
        both = in_order(core, tokens[0], swap(tokens[0]), 0)
        left, right = both[:, :cut], both[:, cut:]
        x_own = jnp.where(core == 0, left, right)
        x_other = jnp.where(core == 0, right, left)
    result = x_own
    for tick in range(section_count):
        acc = project_early(scalars, x_own, w_kv)
        kv, send_pair, send = project_kv(scalars, acc, x_other, w_kv)
        near = to_later_chip(send, 1)
        mid = to_later_chip(send, 2)
        far = to_later_chip(send, 3)
        pair = to_partner_chip(send_pair)
        query, acc, stats = attend_local(scalars, x_own, x_other, w_q, kv)
        att = attend_remote(scalars, query, acc, stats, pair, near, mid, far)
        acc = project_back_early(scalars, x_own, att, w_back)
        produced, result = project_back(scalars, tick, acc, swap(att), w_back, result)
        if tick + 1 < section_count:
            x_own = lax.ppermute(produced, "section", [(tick, tick + 1)])
            x_other = swap(x_own)
    with jax.named_scope("result"):
        top, bottom = result[:128], result[128:]
        mine = jnp.where(core == 0, top, bottom)
        theirs = swap(jnp.where(core == 0, bottom, top))
        return in_order(core, mine, theirs, 1)[None, None]


def solution(mesh):
    return jax.shard_map(
        local,
        mesh=mesh,
        in_specs=(P(None, "seq", None), P("section", "seq", None), P("section", "seq", None), P()),
        out_specs=P("section", None, "seq", None),
        check_vma=False,
    )
```

```python
import functools
import math

import jax
import jax.numpy as jnp
from jax import lax
from jax.experimental import pallas as pl
from jax.experimental.pallas import tpu as pltpu
from jax.sharding import PartitionSpec as P

NEG_FILL = -1e30
HD = 128
CHIP_ROWS = 256
GROUP_CHIPS = 4
BF16 = jnp.bfloat16
F32 = jnp.float32
VMEM_LIMIT = 20 * 1024 * 1024
UNPACK_LIMIT = 46 * 1024 * 1024
PACK_LIMIT = 16 * 1024 * 1024


def dot(a, b):
    return lax.dot_general(a, b, (((1,), (0,)), ((), ())), preferred_element_type=F32)


def dot_t(a, b):
    return lax.dot_general(a, b, (((1,), (1,)), ((), ())), preferred_element_type=F32)


def offset_of(scalars, branch, head_at, heads):
    return scalars[2 + branch * 2 * heads + scalars[0] * heads + head_at]


def rows_of(core, w):
    half = w.shape[0] // 2
    return w[pl.ds(pl.multiple_of(core * half, 128), half), :]


def early_kernel(scalars, own, w, acc):
    acc[...] = dot(own[...], rows_of(scalars[0], w))


def kv_kernel(scalars, acc, other, w, kv_out, pair_out, send_out):
    width = kv_out.shape[1]
    heads = width // (2 * HD)
    kv_out[...] = (acc[...] + dot(other[...], rows_of(1 - scalars[0], w))).astype(BF16)
    row = lax.broadcasted_iota(jnp.int32, (96, CHIP_ROWS), 0)
    col = lax.broadcasted_iota(jnp.int32, (96, CHIP_ROWS), 1)
    for i in range(heads):
        off2 = offset_of(scalars, 2, i, heads)
        off3 = offset_of(scalars, 3, i, heads)
        source = jnp.where(row < 64, 4 * row + off2, 8 * (row - 64) + off3)
        pick = jnp.where(col == source, 1.0, 0.0).astype(BF16)
        cols = slice(2 * i * HD, 2 * (i + 1) * HD)
        picked = dot(pick, kv_out[:, cols]).astype(BF16)
        pair_out[:, cols] = picked[:64]
        send_out[:, cols] = picked[64:]


def with_ones(values):
    return jnp.concatenate([values, jnp.ones_like(values)], axis=1)


def local_kernel(scalars, own, other, w, kv, q_out, acc_out, stat_out):
    width = q_out.shape[1]
    heads = width // HD
    core = scalars[0]
    query = dot(own[...], rows_of(core, w)) + dot(other[...], rows_of(1 - core, w))
    q_out[...] = query.astype(BF16)
    scaling = 1.0 / math.sqrt(HD)
    row = lax.broadcasted_iota(jnp.int32, (CHIP_ROWS, HD), 0)
    lane = lax.broadcasted_iota(jnp.int32, (CHIP_ROWS, HD), 1)
    first = ((lane == 0) & (row < 128)) | ((lane == 1) & (row >= 128))
    period = jnp.where(lane == 2, 1, jnp.where(lane == 3, 3, 7))
    phase = jnp.where((lane >= 2) & (lane <= 4), row & period, -1)
    phase = jnp.where(first, -2, phase)
    causal = []
    for r in range(2):
        shape = (128, 128 * (r + 1))
        causal.append(
            lax.broadcasted_iota(jnp.int32, shape, 1)
            <= lax.broadcasted_iota(jnp.int32, shape, 0) + 128 * r
        )
    lane_half = lax.broadcasted_iota(jnp.int32, (128, HD), 1)
    stats = [jnp.zeros((128, HD), F32) for _ in range(2)]
    work = [(i, r) for i in range(heads) for r in range(2)]
    members = []
    for i in range(heads):
        offset = jnp.where(
            lane == 2,
            offset_of(scalars, 1, i, heads),
            jnp.where(
                lane == 3, offset_of(scalars, 2, i, heads), offset_of(scalars, 3, i, heads)
            ),
        )
        member = (phase == offset) | (phase == -2)
        members.append(jnp.where(member, 1.0, 0.0).astype(BF16))
    times, scores, peaks, expos = {}, {}, {}, {}
    for i, r in work:
        rows = slice(128 * r, 128 * (r + 1))
        seen = slice(0, 128 * (r + 1))
        times[i, r] = jnp.where(causal[r], dot_t(members[i][rows], members[i][seen]), 0.0)
        keys = slice(2 * i * HD, (2 * i + 1) * HD)
        raw = dot_t(q_out[rows, i * HD : (i + 1) * HD], kv[seen, keys]) * scaling
        scores[i, r] = jnp.where(times[i, r] > 0.0, raw, NEG_FILL)
    for at in work:
        peaks[at] = jnp.max(scores[at], axis=1, keepdims=True)
    for at in work:
        expos[at] = times[at] * jnp.exp(scores[at] - peaks[at])
    for i, r in work:
        rows = slice(128 * r, 128 * (r + 1))
        seen = slice(0, 128 * (r + 1))
        vals = slice((2 * i + 1) * HD, (2 * i + 2) * HD)
        acc_out[rows, 2 * i * HD : 2 * (i + 1) * HD] = dot(
            expos[i, r].astype(BF16), with_ones(kv[seen, vals])
        )
        stats[r] = jnp.where(lane_half == i, peaks[i, r], stats[r])
    stat_out[:128] = stats[0]
    stat_out[128:] = stats[1]


def remote_kernel(scalars, query, acc, stat, pair, near, mid, far, out):
    heads = out.shape[1] // HD
    scaling = 1.0 / math.sqrt(HD)
    chip = scalars[1]
    shape = (CHIP_ROWS, 160)
    row = lax.broadcasted_iota(jnp.int32, shape, 0)
    col = lax.broadcasted_iota(jnp.int32, shape, 1)
    second = (col < 64) & ((chip & 1) == 1)
    third = (col >= 64) & (chip >= 1 + (col - 64) // 32)
    row2 = jnp.where(second, row & 3, -1)
    row3 = jnp.where(third, row & 7, -1)
    scores, peaks, expos, mixed = [], [], [], []
    for i in range(heads):
        keys = slice(2 * i * HD, (2 * i + 1) * HD)
        off2 = offset_of(scalars, 2, i, heads)
        off3 = offset_of(scalars, 3, i, heads)
        allowed = (row2 == off2) | (row3 == off3)
        key_rows = jnp.concatenate(
            [pair[:, keys], near[:, keys], mid[:, keys], far[:, keys]], axis=0
        )
        raw = dot_t(query[:, i * HD : (i + 1) * HD], key_rows) * scaling
        scores.append(jnp.where(allowed, raw, NEG_FILL))
    for i in range(heads):
        peaks.append(jnp.maximum(stat[:, i : i + 1], jnp.max(scores[i], axis=1, keepdims=True)))
    for i in range(heads):
        expos.append(jnp.exp(scores[i] - peaks[i]))
    for i in range(heads):
        vals = slice((2 * i + 1) * HD, (2 * i + 2) * HD)
        value_rows = jnp.concatenate(
            [pair[:, vals], near[:, vals], mid[:, vals], far[:, vals]], axis=0
        )
        mixed.append(dot(expos[i].astype(BF16), with_ones(value_rows)))
    for i in range(heads):
        shrink = jnp.exp(stat[:, i : i + 1] - peaks[i])
        both = acc[:, 2 * i * HD : 2 * (i + 1) * HD] * shrink + mixed[i]
        out[:, i * HD : (i + 1) * HD] = (both[:, :HD] / both[:, HD:]).astype(BF16)


def back_early_kernel(scalars, x_own, att_own, w, acc):
    acc[...] = x_own[...].astype(F32) + dot(att_own[...], rows_of(scalars[0], w))


def back_kernel(tick, scalars, acc, att_other, w, earlier, out, result):
    out[...] = (acc[...] + dot(att_other[...], rows_of(1 - scalars[0], w))).astype(BF16)
    mine = scalars[scalars.shape[0] - 1] == tick

    @pl.when(mine)
    def _():
        result[...] = out[...]

    @pl.when(jnp.logical_not(mine))
    def _():
        result[...] = earlier[...]


def pack_kernel(core_ref, w_qkv_hbm, w_out_hbm, own, other, w_qkv, w_out, sems):
    copies = [
        pltpu.make_async_copy(w_qkv_hbm, w_qkv, sems.at[0]),
        pltpu.make_async_copy(w_out_hbm, w_out, sems.at[1]),
    ]
    for copy in copies:
        copy.start()
    third = w_qkv.shape[2] // 3
    width = third // 2
    cut = w_out.shape[2] // 2

    def columns(ref, start, size):
        return ref[0, :, pl.ds(pl.multiple_of(start, 128), size)]

    targets = ((own, core_ref[0]), (other, 1 - core_ref[0]))
    copies[0].wait()
    for target, core in targets:
        for i in range(width // HD):
            start = third + core * width + i * HD
            target[:, 2 * i * HD : (2 * i + 1) * HD] = columns(w_qkv, start, HD)
            target[:, (2 * i + 1) * HD : (2 * i + 2) * HD] = columns(w_qkv, start + third, HD)
        target[:, 2 * width : 3 * width] = columns(w_qkv, core * width, width)
    copies[1].wait()
    for target, core in targets:
        left = columns(w_out, core * cut, width).astype(F32)
        right = columns(w_out, core * cut + width, width).astype(F32)
        target[:, 3 * width :] = jnp.concatenate([left, right], axis=0).astype(BF16)


def join_kernel(core_ref, own, other, block):
    rows = own.shape[0]
    wide = block.shape[1] * 3 // 4
    core = core_ref[0]
    block[pl.ds(pl.multiple_of(core * rows, 16), rows), :wide] = own[:, :wide]
    block[pl.ds(pl.multiple_of((1 - core) * rows, 16), rows), :wide] = other[:, :wide]
    mine, theirs = own[:, wide:].astype(F32), other[:, wide:].astype(F32)
    first = jnp.where(core == 0, mine, theirs)
    second = jnp.where(core == 0, theirs, mine)
    half = rows // 2
    parts = [first[:half], second[:half], first[half:], second[half:]]
    block[:, wide:] = jnp.concatenate(parts, axis=0).astype(BF16)


def unpack_kv_kernel(w, out, sems):
    parts = sems.shape[0]
    rows = out.shape[0] // parts
    copies = []
    for i in range(parts):
        at = pl.ds(i * rows, rows)
        copies.append(
            pltpu.make_async_copy(
                w.at[at, pl.ds(0, out.shape[1])], out.at[at, :], sems.at[i]
            )
        )
    for copy in copies:
        copy.start()
    for copy in copies:
        copy.wait()


def unpack_rest_kernel(w, query, back, query_sems, back_sems):
    width = query.shape[1]
    copies = []
    parts = query_sems.shape[0]
    rows = query.shape[0] // parts
    for i in range(parts):
        at = pl.ds(i * rows, rows)
        copies.append(
            pltpu.make_async_copy(
                w.at[at, pl.ds(2 * width, width)], query.at[at, :], query_sems.at[i]
            )
        )
    chips = back_sems.shape[0] // 2
    rows = back.shape[0] // chips
    for i in range(chips):
        for h in range(2):
            copies.append(
                pltpu.make_async_copy(
                    w.at[pl.ds((2 * i + h) * rows, rows), pl.ds(3 * width, width)],
                    back.at[pl.ds(i * rows, rows), pl.ds(h * width, width)],
                    back_sems.at[2 * i + h],
                )
            )
    for copy in copies:
        copy.start()
    for copy in copies:
        copy.wait()


def unpack(body, w, out_shape, sems):
    return pl.pallas_call(
        body,
        in_specs=[pl.BlockSpec(memory_space=pl.ANY)],
        out_specs=jax.tree.map(lambda _: pl.BlockSpec(memory_space=pltpu.VMEM), out_shape),
        out_shape=out_shape,
        scratch_shapes=[pltpu.SemaphoreType.DMA((count,)) for count in sems],
        compiler_params=pltpu.CompilerParams(vmem_limit_bytes=UNPACK_LIMIT),
    )(w)


def call(body, out_shape, flops, scalars, *operands):
    in_specs = [pl.BlockSpec(memory_space=pltpu.SMEM)]
    in_specs += [pl.BlockSpec(memory_space=pltpu.VMEM) for _ in operands]
    out_specs = jax.tree.map(lambda _: pl.BlockSpec(memory_space=pltpu.VMEM), out_shape)
    return pl.pallas_call(
        body,
        in_specs=in_specs,
        out_specs=out_specs,
        out_shape=out_shape,
        compiler_params=pltpu.CompilerParams(vmem_limit_bytes=VMEM_LIMIT),
        cost_estimate=pl.CostEstimate(flops=flops, bytes_accessed=1, transcendentals=0),
    )(scalars, *operands)


def pack_weights(core, w_qkv, w_out):
    shape = (w_qkv.shape[1], w_qkv.shape[2] * 2 // 3)
    return pl.pallas_call(
        pack_kernel,
        in_specs=[pl.BlockSpec(memory_space=pltpu.SMEM)]
        + [pl.BlockSpec(memory_space=pl.ANY)] * 2,
        out_specs=[pl.BlockSpec(memory_space=pltpu.VMEM)] * 2,
        out_shape=[jax.ShapeDtypeStruct(shape, BF16)] * 2,
        scratch_shapes=[
            pltpu.VMEM(w_qkv.shape, BF16),
            pltpu.VMEM(w_out.shape, BF16),
            pltpu.SemaphoreType.DMA((2,)),
        ],
        compiler_params=pltpu.CompilerParams(vmem_limit_bytes=PACK_LIMIT),
    )(core, w_qkv, w_out)


def join_weights(core, own, other):
    shape = (2 * own.shape[0], own.shape[1])
    return call(join_kernel, jax.ShapeDtypeStruct(shape, BF16), 1, core, own, other)


def project_early(scalars, own, w):
    rows, size = own.shape
    return call(
        early_kernel,
        jax.ShapeDtypeStruct((rows, w.shape[1]), F32),
        2 * rows * size * w.shape[1],
        scalars,
        own,
        w,
    )


def project_kv(scalars, acc, other, w):
    rows, width = acc.shape
    return call(
        kv_kernel,
        [
            jax.ShapeDtypeStruct((rows, width), BF16),
            jax.ShapeDtypeStruct((64, width), BF16),
            jax.ShapeDtypeStruct((32, width), BF16),
        ],
        2 * rows * other.shape[1] * width,
        scalars,
        acc,
        other,
        w,
    )


def attend_local(scalars, own, other, w, kv):
    rows = own.shape[0]
    width = w.shape[1]
    return call(
        local_kernel,
        [
            jax.ShapeDtypeStruct((rows, width), BF16),
            jax.ShapeDtypeStruct((rows, 2 * width), F32),
            jax.ShapeDtypeStruct((rows, HD), F32),
        ],
        4 * rows * (own.shape[1] + 2 * HD) * width,
        scalars,
        own,
        other,
        w,
        kv,
    )


def attend_remote(scalars, query, acc, stats, *sent):
    rows, width = query.shape
    return call(
        remote_kernel,
        jax.ShapeDtypeStruct((rows, width), BF16),
        4 * rows * 160 * width,
        scalars,
        query,
        acc,
        stats,
        *sent,
    )


def last_kernel(tick, scalars, acc, att_other, w, earlier, mine, theirs, result):
    core = scalars[0]
    rows = mine.shape[0]
    is_mine = scalars[scalars.shape[0] - 1] == tick

    @pl.when(is_mine)
    def _():
        part = acc[...] + dot(att_other[...], rows_of(1 - core, w))
        result[...] = part.astype(BF16)

    @pl.when(jnp.logical_not(is_mine))
    def _():
        result[...] = earlier[...]

    mine[...] = result[pl.ds(pl.multiple_of(core * rows, 16), rows), :]
    theirs[...] = result[pl.ds(pl.multiple_of((1 - core) * rows, 16), rows), :]


def project_last(scalars, tick, acc, att_other, w, earlier):
    rows, size = acc.shape
    return pl.pallas_call(
        functools.partial(last_kernel, tick),
        in_specs=[pl.BlockSpec(memory_space=pltpu.SMEM)]
        + [pl.BlockSpec(memory_space=pltpu.VMEM)] * 4,
        out_specs=[pl.BlockSpec(memory_space=pltpu.VMEM)] * 2,
        out_shape=[jax.ShapeDtypeStruct((rows // 2, size), BF16)] * 2,
        scratch_shapes=[pltpu.VMEM((rows, size), BF16)],
        compiler_params=pltpu.CompilerParams(vmem_limit_bytes=VMEM_LIMIT),
    )(scalars, acc, att_other, w, earlier)


def project_back_early(scalars, x_own, att_own, w):
    rows, size = x_own.shape
    return call(
        back_early_kernel,
        jax.ShapeDtypeStruct((rows, size), F32),
        2 * rows * size * att_own.shape[1],
        scalars,
        x_own,
        att_own,
        w,
    )


def project_back(scalars, tick, acc, att_other, w, earlier):
    rows, size = acc.shape
    return call(
        functools.partial(back_kernel, tick),
        [jax.ShapeDtypeStruct((rows, size), BF16)] * 2,
        2 * rows * size * att_other.shape[1],
        scalars,
        acc,
        att_other,
        w,
        earlier,
    )


def swap(value):
    count = lax.axis_size("seq")
    return lax.ppermute(value, "seq", [(i, i ^ 1) for i in range(count)])


def to_later_chip(value, steps):
    count = lax.axis_size("seq")
    pairs = []
    for source in range(count):
        if (source // 2) % GROUP_CHIPS + steps < GROUP_CHIPS:
            pairs.append((source, source + 2 * steps))
    return lax.ppermute(value, "seq", pairs)


def to_partner_chip(value):
    count = lax.axis_size("seq")
    pairs = [(source, source + 2) for source in range(count) if (source // 2) % 2 == 0]
    return lax.ppermute(value, "seq", pairs)


def in_order(core, own, other, axis):
    return jnp.where(
        core == 0,
        jnp.concatenate([own, other], axis=axis),
        jnp.concatenate([other, own], axis=axis),
    )


def gather_chips(block):
    count = lax.axis_size("seq")
    groups = [list(range(core, count, 2)) for core in range(2)]
    return lax.all_gather(block, "seq", axis=0, tiled=True, axis_index_groups=groups)


def local(tokens, w_qkv, w_out, offsets):
    section = lax.axis_index("section")
    section_count = lax.axis_size("section")
    seq = lax.axis_index("seq")
    core = seq % 2
    scalars = jnp.concatenate(
        [
            jnp.stack([core, (seq // 2) % GROUP_CHIPS]).astype(jnp.int32),
            offsets.reshape(-1).astype(jnp.int32),
            jnp.full((1,), section, jnp.int32),
        ]
    )
    with jax.named_scope("weights"):
        rows = w_qkv.shape[1]
        width = w_qkv.shape[2] // 6
        cut = w_out.shape[2] // 2
        core_array = jnp.full((1,), core, jnp.int32)
        own, other = pack_weights(core_array, w_qkv, w_out)
        block = join_weights(core_array, own, swap(other))
        block, tokens = lax.optimization_barrier((block, tokens))
        w_all = gather_chips(block)
        depth = w_all.shape[0]
        w_kv = unpack(
            unpack_kv_kernel, w_all, jax.ShapeDtypeStruct((depth, 2 * width), BF16), [8]
        )
        w_q, w_back = unpack(
            unpack_rest_kernel,
            w_all,
            [
                jax.ShapeDtypeStruct((depth, width), BF16),
                jax.ShapeDtypeStruct((depth // 2, cut), BF16),
            ],
            [8, depth // rows],
        )
    with jax.named_scope("tokens"):
        both = in_order(core, tokens[0], swap(tokens[0]), 0)
        left, right = both[:, :cut], both[:, cut:]
        x_own = jnp.where(core == 0, left, right)
        x_other = jnp.where(core == 0, right, left)
    result = x_own
    for tick in range(section_count):
        acc = project_early(scalars, x_own, w_kv)
        kv, send_pair, send = project_kv(scalars, acc, x_other, w_kv)
        near = to_later_chip(send, 1)
        mid = to_later_chip(send, 2)
        far = to_later_chip(send, 3)
        pair = to_partner_chip(send_pair)
        query, acc, stats = attend_local(scalars, x_own, x_other, w_q, kv)
        att = attend_remote(scalars, query, acc, stats, pair, near, mid, far)
        acc = project_back_early(scalars, x_own, att, w_back)
        if tick + 1 < section_count:
            produced, result = project_back(scalars, tick, acc, swap(att), w_back, result)
        else:
            mine, theirs = project_last(scalars, tick, acc, swap(att), w_back, result)
        if tick + 1 < section_count:
            x_own = lax.ppermute(produced, "section", [(tick, tick + 1)])
            x_other = swap(x_own)
    with jax.named_scope("result"):
        theirs = swap(theirs)
        return in_order(core, mine, theirs, 1)[None, None]


def solution(mesh):
    return jax.shard_map(
        local,
        mesh=mesh,
        in_specs=(P(None, "seq", None), P("section", "seq", None), P("section", "seq", None), P()),
        out_specs=P("section", None, "seq", None),
        check_vma=False,
    )
```

```python
import functools
import math

import jax
import jax.numpy as jnp
from jax import lax
from jax.experimental import pallas as pl
from jax.experimental.pallas import tpu as pltpu
from jax.sharding import PartitionSpec as P

NEG_FILL = -1e30
HD = 128
CHIP_ROWS = 256
GROUP_CHIPS = 4
BF16 = jnp.bfloat16
F32 = jnp.float32
VMEM_LIMIT = 20 * 1024 * 1024
UNPACK_LIMIT = 46 * 1024 * 1024
PACK_LIMIT = 16 * 1024 * 1024


def dot(a, b):
    return lax.dot_general(a, b, (((1,), (0,)), ((), ())), preferred_element_type=F32)


def dot_t(a, b):
    return lax.dot_general(a, b, (((1,), (1,)), ((), ())), preferred_element_type=F32)


def offset_of(scalars, branch, head_at, heads):
    return scalars[2 + branch * 2 * heads + scalars[0] * heads + head_at]


def rows_of(core, w):
    half = w.shape[0] // 2
    return w[pl.ds(pl.multiple_of(core * half, 128), half), :]


def early_kernel(scalars, own, w, acc):
    acc[...] = dot(own[...], rows_of(scalars[0], w))


def kv_kernel(scalars, acc, other, w, kv_out, pair_out, send_out):
    width = kv_out.shape[1]
    heads = width // (2 * HD)
    kv_out[...] = (acc[...] + dot(other[...], rows_of(1 - scalars[0], w))).astype(BF16)
    row = lax.broadcasted_iota(jnp.int32, (96, CHIP_ROWS), 0)
    col = lax.broadcasted_iota(jnp.int32, (96, CHIP_ROWS), 1)
    for i in range(heads):
        off2 = offset_of(scalars, 2, i, heads)
        off3 = offset_of(scalars, 3, i, heads)
        source = jnp.where(row < 64, 4 * row + off2, 8 * (row - 64) + off3)
        pick = jnp.where(col == source, 1.0, 0.0).astype(BF16)
        cols = slice(2 * i * HD, 2 * (i + 1) * HD)
        picked = dot(pick, kv_out[:, cols]).astype(BF16)
        pair_out[:, cols] = picked
        send_out[:, cols] = picked[64:]


def with_ones(values):
    return jnp.concatenate([values, jnp.ones_like(values)], axis=1)


def local_kernel(scalars, own, other, w, kv, q_out, acc_out, stat_out):
    width = q_out.shape[1]
    heads = width // HD
    core = scalars[0]
    query = dot(own[...], rows_of(core, w)) + dot(other[...], rows_of(1 - core, w))
    q_out[...] = query.astype(BF16)
    scaling = 1.0 / math.sqrt(HD)
    row = lax.broadcasted_iota(jnp.int32, (CHIP_ROWS, HD), 0)
    lane = lax.broadcasted_iota(jnp.int32, (CHIP_ROWS, HD), 1)
    first = ((lane == 0) & (row < 128)) | ((lane == 1) & (row >= 128))
    period = jnp.where(lane == 2, 1, jnp.where(lane == 3, 3, 7))
    phase = jnp.where((lane >= 2) & (lane <= 4), row & period, -1)
    phase = jnp.where(first, -2, phase)
    causal = []
    for r in range(2):
        shape = (128, 128 * (r + 1))
        causal.append(
            lax.broadcasted_iota(jnp.int32, shape, 1)
            <= lax.broadcasted_iota(jnp.int32, shape, 0) + 128 * r
        )
    lane_half = lax.broadcasted_iota(jnp.int32, (128, HD), 1)
    stats = [jnp.zeros((128, HD), F32) for _ in range(2)]
    work = [(i, r) for i in range(heads) for r in range(2)]
    members = []
    for i in range(heads):
        offset = jnp.where(
            lane == 2,
            offset_of(scalars, 1, i, heads),
            jnp.where(
                lane == 3, offset_of(scalars, 2, i, heads), offset_of(scalars, 3, i, heads)
            ),
        )
        member = (phase == offset) | (phase == -2)
        members.append(jnp.where(member, 1.0, 0.0).astype(BF16))
    times, scores, peaks, expos = {}, {}, {}, {}
    for i, r in work:
        rows = slice(128 * r, 128 * (r + 1))
        seen = slice(0, 128 * (r + 1))
        times[i, r] = jnp.where(causal[r], dot_t(members[i][rows], members[i][seen]), 0.0)
        keys = slice(2 * i * HD, (2 * i + 1) * HD)
        raw = dot_t(q_out[rows, i * HD : (i + 1) * HD], kv[seen, keys]) * scaling
        scores[i, r] = jnp.where(times[i, r] > 0.0, raw, NEG_FILL)
    for at in work:
        peaks[at] = jnp.max(scores[at], axis=1, keepdims=True)
    for at in work:
        expos[at] = times[at] * jnp.exp(scores[at] - peaks[at])
    for i, r in work:
        rows = slice(128 * r, 128 * (r + 1))
        seen = slice(0, 128 * (r + 1))
        vals = slice((2 * i + 1) * HD, (2 * i + 2) * HD)
        acc_out[rows, 2 * i * HD : 2 * (i + 1) * HD] = dot(
            expos[i, r].astype(BF16), with_ones(kv[seen, vals])
        )
        stats[r] = jnp.where(lane_half == i, peaks[i, r], stats[r])
    stat_out[:128] = stats[0]
    stat_out[128:] = stats[1]


def remote_kernel(scalars, query, acc, stat, pair, mid, cross, out):
    heads = out.shape[1] // HD
    scaling = 1.0 / math.sqrt(HD)
    chip = scalars[1]
    shape = (CHIP_ROWS, 160)
    row = lax.broadcasted_iota(jnp.int32, shape, 0)
    col = lax.broadcasted_iota(jnp.int32, shape, 1)
    odd = (chip & 1) == 1
    second = (col < 64) & odd
    third = ((col >= 64) & (col < 96) & odd) | ((col >= 96) & (chip >= 2))
    row2 = jnp.where(second, row & 3, -1)
    row3 = jnp.where(third, row & 7, -1)
    scores, peaks, expos, mixed = [], [], [], []
    for i in range(heads):
        keys = slice(2 * i * HD, (2 * i + 1) * HD)
        off2 = offset_of(scalars, 2, i, heads)
        off3 = offset_of(scalars, 3, i, heads)
        allowed = (row2 == off2) | (row3 == off3)
        key_rows = jnp.concatenate(
            [pair[:, keys], mid[:, keys], cross[:, keys]], axis=0
        )
        raw = dot_t(query[:, i * HD : (i + 1) * HD], key_rows) * scaling
        scores.append(jnp.where(allowed, raw, NEG_FILL))
    for i in range(heads):
        peaks.append(jnp.maximum(stat[:, i : i + 1], jnp.max(scores[i], axis=1, keepdims=True)))
    for i in range(heads):
        expos.append(jnp.exp(scores[i] - peaks[i]))
    for i in range(heads):
        vals = slice((2 * i + 1) * HD, (2 * i + 2) * HD)
        value_rows = jnp.concatenate(
            [pair[:, vals], mid[:, vals], cross[:, vals]], axis=0
        )
        mixed.append(dot(expos[i].astype(BF16), with_ones(value_rows)))
    for i in range(heads):
        shrink = jnp.exp(stat[:, i : i + 1] - peaks[i])
        both = acc[:, 2 * i * HD : 2 * (i + 1) * HD] * shrink + mixed[i]
        out[:, i * HD : (i + 1) * HD] = (both[:, :HD] / both[:, HD:]).astype(BF16)


def back_early_kernel(scalars, x_own, att_own, w, acc):
    acc[...] = x_own[...].astype(F32) + dot(att_own[...], rows_of(scalars[0], w))


def back_kernel(tick, scalars, acc, att_other, w, earlier, out, result):
    out[...] = (acc[...] + dot(att_other[...], rows_of(1 - scalars[0], w))).astype(BF16)
    mine = scalars[scalars.shape[0] - 1] == tick

    @pl.when(mine)
    def _():
        result[...] = out[...]

    @pl.when(jnp.logical_not(mine))
    def _():
        result[...] = earlier[...]


def pack_kernel(core_ref, w_qkv_hbm, w_out_hbm, own, other, w_qkv, w_out, sems):
    copies = [
        pltpu.make_async_copy(w_qkv_hbm, w_qkv, sems.at[0]),
        pltpu.make_async_copy(w_out_hbm, w_out, sems.at[1]),
    ]
    for copy in copies:
        copy.start()
    third = w_qkv.shape[2] // 3
    width = third // 2
    cut = w_out.shape[2] // 2

    def columns(ref, start, size):
        return ref[0, :, pl.ds(pl.multiple_of(start, 128), size)]

    targets = ((own, core_ref[0]), (other, 1 - core_ref[0]))
    copies[0].wait()
    for target, core in targets:
        for i in range(width // HD):
            start = third + core * width + i * HD
            target[:, 2 * i * HD : (2 * i + 1) * HD] = columns(w_qkv, start, HD)
            target[:, (2 * i + 1) * HD : (2 * i + 2) * HD] = columns(w_qkv, start + third, HD)
        target[:, 2 * width : 3 * width] = columns(w_qkv, core * width, width)
    copies[1].wait()
    for target, core in targets:
        left = columns(w_out, core * cut, width).astype(F32)
        right = columns(w_out, core * cut + width, width).astype(F32)
        target[:, 3 * width :] = jnp.concatenate([left, right], axis=0).astype(BF16)


def join_kernel(core_ref, own, other, block):
    rows = own.shape[0]
    wide = block.shape[1] * 3 // 4
    core = core_ref[0]
    block[pl.ds(pl.multiple_of(core * rows, 16), rows), :wide] = own[:, :wide]
    block[pl.ds(pl.multiple_of((1 - core) * rows, 16), rows), :wide] = other[:, :wide]
    mine, theirs = own[:, wide:].astype(F32), other[:, wide:].astype(F32)
    first = jnp.where(core == 0, mine, theirs)
    second = jnp.where(core == 0, theirs, mine)
    half = rows // 2
    parts = [first[:half], second[:half], first[half:], second[half:]]
    block[:, wide:] = jnp.concatenate(parts, axis=0).astype(BF16)


def unpack_kv_kernel(w, out, sems):
    parts = sems.shape[0]
    rows = out.shape[0] // parts
    copies = []
    for i in range(parts):
        at = pl.ds(i * rows, rows)
        copies.append(
            pltpu.make_async_copy(
                w.at[at, pl.ds(0, out.shape[1])], out.at[at, :], sems.at[i]
            )
        )
    for copy in copies:
        copy.start()
    for copy in copies:
        copy.wait()


def unpack_rest_kernel(w, query, back, query_sems, back_sems):
    width = query.shape[1]
    copies = []
    parts = query_sems.shape[0]
    rows = query.shape[0] // parts
    for i in range(parts):
        at = pl.ds(i * rows, rows)
        copies.append(
            pltpu.make_async_copy(
                w.at[at, pl.ds(2 * width, width)], query.at[at, :], query_sems.at[i]
            )
        )
    chips = back_sems.shape[0] // 2
    rows = back.shape[0] // chips
    for i in range(chips):
        for h in range(2):
            copies.append(
                pltpu.make_async_copy(
                    w.at[pl.ds((2 * i + h) * rows, rows), pl.ds(3 * width, width)],
                    back.at[pl.ds(i * rows, rows), pl.ds(h * width, width)],
                    back_sems.at[2 * i + h],
                )
            )
    for copy in copies:
        copy.start()
    for copy in copies:
        copy.wait()


def unpack(body, w, out_shape, sems):
    return pl.pallas_call(
        body,
        in_specs=[pl.BlockSpec(memory_space=pl.ANY)],
        out_specs=jax.tree.map(lambda _: pl.BlockSpec(memory_space=pltpu.VMEM), out_shape),
        out_shape=out_shape,
        scratch_shapes=[pltpu.SemaphoreType.DMA((count,)) for count in sems],
        compiler_params=pltpu.CompilerParams(vmem_limit_bytes=UNPACK_LIMIT),
    )(w)


def call(body, out_shape, flops, scalars, *operands):
    in_specs = [pl.BlockSpec(memory_space=pltpu.SMEM)]
    in_specs += [pl.BlockSpec(memory_space=pltpu.VMEM) for _ in operands]
    out_specs = jax.tree.map(lambda _: pl.BlockSpec(memory_space=pltpu.VMEM), out_shape)
    return pl.pallas_call(
        body,
        in_specs=in_specs,
        out_specs=out_specs,
        out_shape=out_shape,
        compiler_params=pltpu.CompilerParams(vmem_limit_bytes=VMEM_LIMIT),
        cost_estimate=pl.CostEstimate(flops=flops, bytes_accessed=1, transcendentals=0),
    )(scalars, *operands)


def pack_weights(core, w_qkv, w_out):
    shape = (w_qkv.shape[1], w_qkv.shape[2] * 2 // 3)
    return pl.pallas_call(
        pack_kernel,
        in_specs=[pl.BlockSpec(memory_space=pltpu.SMEM)]
        + [pl.BlockSpec(memory_space=pl.ANY)] * 2,
        out_specs=[pl.BlockSpec(memory_space=pltpu.VMEM)] * 2,
        out_shape=[jax.ShapeDtypeStruct(shape, BF16)] * 2,
        scratch_shapes=[
            pltpu.VMEM(w_qkv.shape, BF16),
            pltpu.VMEM(w_out.shape, BF16),
            pltpu.SemaphoreType.DMA((2,)),
        ],
        compiler_params=pltpu.CompilerParams(vmem_limit_bytes=PACK_LIMIT),
    )(core, w_qkv, w_out)


def join_weights(core, own, other):
    shape = (2 * own.shape[0], own.shape[1])
    return call(join_kernel, jax.ShapeDtypeStruct(shape, BF16), 1, core, own, other)


def project_early(scalars, own, w):
    rows, size = own.shape
    return call(
        early_kernel,
        jax.ShapeDtypeStruct((rows, w.shape[1]), F32),
        2 * rows * size * w.shape[1],
        scalars,
        own,
        w,
    )


def project_kv(scalars, acc, other, w):
    rows, width = acc.shape
    return call(
        kv_kernel,
        [
            jax.ShapeDtypeStruct((rows, width), BF16),
            jax.ShapeDtypeStruct((96, width), BF16),
            jax.ShapeDtypeStruct((32, width), BF16),
        ],
        2 * rows * other.shape[1] * width,
        scalars,
        acc,
        other,
        w,
    )


def attend_local(scalars, own, other, w, kv):
    rows = own.shape[0]
    width = w.shape[1]
    return call(
        local_kernel,
        [
            jax.ShapeDtypeStruct((rows, width), BF16),
            jax.ShapeDtypeStruct((rows, 2 * width), F32),
            jax.ShapeDtypeStruct((rows, HD), F32),
        ],
        4 * rows * (own.shape[1] + 2 * HD) * width,
        scalars,
        own,
        other,
        w,
        kv,
    )


def attend_remote(scalars, query, acc, stats, *sent):
    rows, width = query.shape
    return call(
        remote_kernel,
        jax.ShapeDtypeStruct((rows, width), BF16),
        4 * rows * 160 * width,
        scalars,
        query,
        acc,
        stats,
        *sent,
    )


def last_kernel(tick, scalars, acc, att_other, w, earlier, mine, theirs, result):
    core = scalars[0]
    rows = mine.shape[0]
    is_mine = scalars[scalars.shape[0] - 1] == tick

    @pl.when(is_mine)
    def _():
        part = acc[...] + dot(att_other[...], rows_of(1 - core, w))
        result[...] = part.astype(BF16)

    @pl.when(jnp.logical_not(is_mine))
    def _():
        result[...] = earlier[...]

    mine[...] = result[pl.ds(pl.multiple_of(core * rows, 16), rows), :]
    theirs[...] = result[pl.ds(pl.multiple_of((1 - core) * rows, 16), rows), :]


def project_last(scalars, tick, acc, att_other, w, earlier):
    rows, size = acc.shape
    return pl.pallas_call(
        functools.partial(last_kernel, tick),
        in_specs=[pl.BlockSpec(memory_space=pltpu.SMEM)]
        + [pl.BlockSpec(memory_space=pltpu.VMEM)] * 4,
        out_specs=[pl.BlockSpec(memory_space=pltpu.VMEM)] * 2,
        out_shape=[jax.ShapeDtypeStruct((rows // 2, size), BF16)] * 2,
        scratch_shapes=[pltpu.VMEM((rows, size), BF16)],
        compiler_params=pltpu.CompilerParams(vmem_limit_bytes=VMEM_LIMIT),
    )(scalars, acc, att_other, w, earlier)


def project_back_early(scalars, x_own, att_own, w):
    rows, size = x_own.shape
    return call(
        back_early_kernel,
        jax.ShapeDtypeStruct((rows, size), F32),
        2 * rows * size * att_own.shape[1],
        scalars,
        x_own,
        att_own,
        w,
    )


def project_back(scalars, tick, acc, att_other, w, earlier):
    rows, size = acc.shape
    return call(
        functools.partial(back_kernel, tick),
        [jax.ShapeDtypeStruct((rows, size), BF16)] * 2,
        2 * rows * size * att_other.shape[1],
        scalars,
        acc,
        att_other,
        w,
        earlier,
    )


def swap(value):
    count = lax.axis_size("seq")
    return lax.ppermute(value, "seq", [(i, i ^ 1) for i in range(count)])


def to_chips(value, moves):
    count = lax.axis_size("seq")
    step = 2 * GROUP_CHIPS
    pairs = [
        (first + 2 * source + core, first + 2 * target + core)
        for first in range(0, count, step)
        for source, target in moves
        for core in range(2)
    ]
    return lax.ppermute(value, "seq", pairs)


def in_order(core, own, other, axis):
    return jnp.where(
        core == 0,
        jnp.concatenate([own, other], axis=axis),
        jnp.concatenate([other, own], axis=axis),
    )


def gather_chips(block):
    count = lax.axis_size("seq")
    groups = [list(range(core, count, 2)) for core in range(2)]
    return lax.all_gather(block, "seq", axis=0, tiled=True, axis_index_groups=groups)


def local(tokens, w_qkv, w_out, offsets):
    section = lax.axis_index("section")
    section_count = lax.axis_size("section")
    seq = lax.axis_index("seq")
    core = seq % 2
    scalars = jnp.concatenate(
        [
            jnp.stack([core, (seq // 2) % GROUP_CHIPS]).astype(jnp.int32),
            offsets.reshape(-1).astype(jnp.int32),
            jnp.full((1,), section, jnp.int32),
        ]
    )
    with jax.named_scope("weights"):
        rows = w_qkv.shape[1]
        width = w_qkv.shape[2] // 6
        cut = w_out.shape[2] // 2
        core_array = jnp.full((1,), core, jnp.int32)
        own, other = pack_weights(core_array, w_qkv, w_out)
        block = join_weights(core_array, own, swap(other))
        block, tokens = lax.optimization_barrier((block, tokens))
        w_all = gather_chips(block)
        depth = w_all.shape[0]
        w_kv = unpack(
            unpack_kv_kernel, w_all, jax.ShapeDtypeStruct((depth, 2 * width), BF16), [8]
        )
        w_q, w_back = unpack(
            unpack_rest_kernel,
            w_all,
            [
                jax.ShapeDtypeStruct((depth, width), BF16),
                jax.ShapeDtypeStruct((depth // 2, cut), BF16),
            ],
            [8, depth // rows],
        )
    with jax.named_scope("tokens"):
        both = in_order(core, tokens[0], swap(tokens[0]), 0)
        left, right = both[:, :cut], both[:, cut:]
        x_own = jnp.where(core == 0, left, right)
        x_other = jnp.where(core == 0, right, left)
    result = x_own
    for tick in range(section_count):
        acc = project_early(scalars, x_own, w_kv)
        kv, send_pair, send = project_kv(scalars, acc, x_other, w_kv)
        cross = to_chips(send, ((0, 3), (1, 2)))
        mid = to_chips(send, ((0, 2), (1, 3)))
        pair = to_chips(send_pair, ((0, 1), (2, 3)))
        query, acc, stats = attend_local(scalars, x_own, x_other, w_q, kv)
        att = attend_remote(scalars, query, acc, stats, pair, mid, cross)
        acc = project_back_early(scalars, x_own, att, w_back)
        if tick + 1 < section_count:
            produced, result = project_back(scalars, tick, acc, swap(att), w_back, result)
        else:
            mine, theirs = project_last(scalars, tick, acc, swap(att), w_back, result)
        if tick + 1 < section_count:
            x_own = lax.ppermute(produced, "section", [(tick, tick + 1)])
            x_other = swap(x_own)
    with jax.named_scope("result"):
        theirs = swap(theirs)
        return in_order(core, mine, theirs, 1)[None, None]


def solution(mesh):
    return jax.shard_map(
        local,
        mesh=mesh,
        in_specs=(P(None, "seq", None), P("section", "seq", None), P("section", "seq", None), P()),
        out_specs=P("section", None, "seq", None),
        check_vma=False,
    )
```

```python
import functools
import math

import jax
import jax.numpy as jnp
from jax import lax
from jax.experimental import pallas as pl
from jax.experimental.pallas import tpu as pltpu
from jax.sharding import PartitionSpec as P

NEG_FILL = -1e30
HD = 128
CHIP_ROWS = 256
GROUP_CHIPS = 4
BF16 = jnp.bfloat16
F32 = jnp.float32
VMEM_LIMIT = 20 * 1024 * 1024
UNPACK_LIMIT = 46 * 1024 * 1024
PACK_LIMIT = 16 * 1024 * 1024


def dot(a, b):
    return lax.dot_general(a, b, (((1,), (0,)), ((), ())), preferred_element_type=F32)


def dot_t(a, b):
    return lax.dot_general(a, b, (((1,), (1,)), ((), ())), preferred_element_type=F32)


def offset_of(scalars, branch, head_at, heads):
    return scalars[2 + branch * 2 * heads + scalars[0] * heads + head_at]


def rows_of(core, w):
    half = w.shape[0] // 2
    return w[pl.ds(pl.multiple_of(core * half, 128), half), :]


def early_kernel(scalars, own, w, acc):
    acc[...] = dot(own[...], rows_of(scalars[0], w))


def kv_kernel(scalars, acc, other, w, kv_out, pair_out, send_out):
    width = kv_out.shape[1]
    heads = width // (2 * HD)
    kv_out[...] = (acc[...] + dot(other[...], rows_of(1 - scalars[0], w))).astype(BF16)
    row = lax.broadcasted_iota(jnp.int32, (96, CHIP_ROWS), 0)
    col = lax.broadcasted_iota(jnp.int32, (96, CHIP_ROWS), 1)
    for i in range(heads):
        off2 = offset_of(scalars, 2, i, heads)
        off3 = offset_of(scalars, 3, i, heads)
        source = jnp.where(row < 64, 4 * row + off2, 8 * (row - 64) + off3)
        pick = jnp.where(col == source, 1.0, 0.0).astype(BF16)
        cols = slice(2 * i * HD, 2 * (i + 1) * HD)
        picked = dot(pick, kv_out[:, cols]).astype(BF16)
        pair_out[:, cols] = picked
        send_out[:, cols] = picked[64:]


def with_ones(values):
    return jnp.concatenate([values, jnp.ones_like(values)], axis=1)


def local_kernel(scalars, own, other, w, kv, q_out, acc_out, stat_out):
    width = q_out.shape[1]
    heads = width // HD
    core = scalars[0]
    query = dot(own[...], rows_of(core, w)) + dot(other[...], rows_of(1 - core, w))
    q_out[...] = query.astype(BF16)
    scaling = 1.0 / math.sqrt(HD)
    row = lax.broadcasted_iota(jnp.int32, (CHIP_ROWS, HD), 0)
    lane = lax.broadcasted_iota(jnp.int32, (CHIP_ROWS, HD), 1)
    first = ((lane == 0) & (row < 128)) | ((lane == 1) & (row >= 128))
    period = jnp.where(lane == 2, 1, jnp.where(lane == 3, 3, 7))
    phase = jnp.where((lane >= 2) & (lane <= 4), row & period, -1)
    phase = jnp.where(first, -2, phase)
    causal = []
    for r in range(2):
        shape = (128, 128 * (r + 1))
        causal.append(
            lax.broadcasted_iota(jnp.int32, shape, 1)
            <= lax.broadcasted_iota(jnp.int32, shape, 0) + 128 * r
        )
    lane_half = lax.broadcasted_iota(jnp.int32, (128, HD), 1)
    stats = [jnp.zeros((128, HD), F32) for _ in range(2)]
    work = [(i, r) for i in range(heads) for r in range(2)]
    members = []
    for i in range(heads):
        offset = jnp.where(
            lane == 2,
            offset_of(scalars, 1, i, heads),
            jnp.where(
                lane == 3, offset_of(scalars, 2, i, heads), offset_of(scalars, 3, i, heads)
            ),
        )
        member = (phase == offset) | (phase == -2)
        members.append(jnp.where(member, 1.0, 0.0).astype(BF16))
    times, scores, peaks, expos = {}, {}, {}, {}
    for i, r in work:
        rows = slice(128 * r, 128 * (r + 1))
        seen = slice(0, 128 * (r + 1))
        times[i, r] = jnp.where(causal[r], dot_t(members[i][rows], members[i][seen]), 0.0)
        keys = slice(2 * i * HD, (2 * i + 1) * HD)
        raw = dot_t(q_out[rows, i * HD : (i + 1) * HD], kv[seen, keys]) * scaling
        scores[i, r] = jnp.where(times[i, r] > 0.0, raw, NEG_FILL)
    for at in work:
        peaks[at] = jnp.max(scores[at], axis=1, keepdims=True)
    for at in work:
        expos[at] = times[at] * jnp.exp(scores[at] - peaks[at])
    for i, r in work:
        rows = slice(128 * r, 128 * (r + 1))
        seen = slice(0, 128 * (r + 1))
        vals = slice((2 * i + 1) * HD, (2 * i + 2) * HD)
        acc_out[rows, 2 * i * HD : 2 * (i + 1) * HD] = dot(
            expos[i, r].astype(BF16), with_ones(kv[seen, vals])
        )
        stats[r] = jnp.where(lane_half == i, peaks[i, r], stats[r])
    stat_out[:128] = stats[0]
    stat_out[128:] = stats[1]


def remote_kernel(scalars, query, acc, stat, pair, mid, cross, out):
    heads = out.shape[1] // HD
    scaling = 1.0 / math.sqrt(HD)
    chip = scalars[1]

    @pl.when(chip == 0)
    def _():
        for i in range(heads):
            both = acc[:, 2 * i * HD : 2 * (i + 1) * HD]
            out[:, i * HD : (i + 1) * HD] = (both[:, :HD] / both[:, HD:]).astype(BF16)

    @pl.when(chip > 0)
    def _():
        shape = (CHIP_ROWS, 160)
        row = lax.broadcasted_iota(jnp.int32, shape, 0)
        col = lax.broadcasted_iota(jnp.int32, shape, 1)
        odd = (chip & 1) == 1
        second = (col < 64) & odd
        third = ((col >= 64) & (col < 96) & odd) | ((col >= 96) & (chip >= 2))
        row2 = jnp.where(second, row & 3, -1)
        row3 = jnp.where(third, row & 7, -1)
        scores, peaks, expos, mixed = [], [], [], []
        for i in range(heads):
            keys = slice(2 * i * HD, (2 * i + 1) * HD)
            off2 = offset_of(scalars, 2, i, heads)
            off3 = offset_of(scalars, 3, i, heads)
            allowed = (row2 == off2) | (row3 == off3)
            key_rows = jnp.concatenate(
                [pair[:, keys], mid[:, keys], cross[:, keys]], axis=0
            )
            raw = dot_t(query[:, i * HD : (i + 1) * HD], key_rows) * scaling
            scores.append(jnp.where(allowed, raw, NEG_FILL))
        for i in range(heads):
            peaks.append(jnp.maximum(stat[:, i : i + 1], jnp.max(scores[i], axis=1, keepdims=True)))
        for i in range(heads):
            expos.append(jnp.exp(scores[i] - peaks[i]))
        for i in range(heads):
            vals = slice((2 * i + 1) * HD, (2 * i + 2) * HD)
            value_rows = jnp.concatenate(
                [pair[:, vals], mid[:, vals], cross[:, vals]], axis=0
            )
            mixed.append(dot(expos[i].astype(BF16), with_ones(value_rows)))
        for i in range(heads):
            shrink = jnp.exp(stat[:, i : i + 1] - peaks[i])
            both = acc[:, 2 * i * HD : 2 * (i + 1) * HD] * shrink + mixed[i]
            out[:, i * HD : (i + 1) * HD] = (both[:, :HD] / both[:, HD:]).astype(BF16)


def back_early_kernel(scalars, x_own, att_own, w, acc):
    acc[...] = x_own[...].astype(F32) + dot(att_own[...], rows_of(scalars[0], w))


def back_kernel(tick, scalars, acc, att_other, w, earlier, out, result):
    out[...] = (acc[...] + dot(att_other[...], rows_of(1 - scalars[0], w))).astype(BF16)
    mine = scalars[scalars.shape[0] - 1] == tick

    @pl.when(mine)
    def _():
        result[...] = out[...]

    @pl.when(jnp.logical_not(mine))
    def _():
        result[...] = earlier[...]


def pack_kernel(core_ref, w_qkv_hbm, w_out_hbm, own, other, w_qkv, w_out, sems):
    copies = [
        pltpu.make_async_copy(w_qkv_hbm, w_qkv, sems.at[0]),
        pltpu.make_async_copy(w_out_hbm, w_out, sems.at[1]),
    ]
    for copy in copies:
        copy.start()
    third = w_qkv.shape[2] // 3
    width = third // 2
    cut = w_out.shape[2] // 2

    def columns(ref, start, size):
        return ref[0, :, pl.ds(pl.multiple_of(start, 128), size)]

    targets = ((own, core_ref[0]), (other, 1 - core_ref[0]))
    copies[0].wait()
    for target, core in targets:
        for i in range(width // HD):
            start = third + core * width + i * HD
            target[:, 2 * i * HD : (2 * i + 1) * HD] = columns(w_qkv, start, HD)
            target[:, (2 * i + 1) * HD : (2 * i + 2) * HD] = columns(w_qkv, start + third, HD)
        target[:, 2 * width : 3 * width] = columns(w_qkv, core * width, width)
    copies[1].wait()
    for target, core in targets:
        left = columns(w_out, core * cut, width).astype(F32)
        right = columns(w_out, core * cut + width, width).astype(F32)
        target[:, 3 * width :] = jnp.concatenate([left, right], axis=0).astype(BF16)


def join_kernel(core_ref, own, other, block):
    rows = own.shape[0]
    wide = block.shape[1] * 3 // 4
    core = core_ref[0]
    block[pl.ds(pl.multiple_of(core * rows, 16), rows), :wide] = own[:, :wide]
    block[pl.ds(pl.multiple_of((1 - core) * rows, 16), rows), :wide] = other[:, :wide]
    mine, theirs = own[:, wide:].astype(F32), other[:, wide:].astype(F32)
    first = jnp.where(core == 0, mine, theirs)
    second = jnp.where(core == 0, theirs, mine)
    half = rows // 2
    parts = [first[:half], second[:half], first[half:], second[half:]]
    block[:, wide:] = jnp.concatenate(parts, axis=0).astype(BF16)


def unpack_kv_kernel(w, out, sems):
    parts = sems.shape[0]
    rows = out.shape[0] // parts
    copies = []
    for i in range(parts):
        at = pl.ds(i * rows, rows)
        copies.append(
            pltpu.make_async_copy(
                w.at[at, pl.ds(0, out.shape[1])], out.at[at, :], sems.at[i]
            )
        )
    for copy in copies:
        copy.start()
    for copy in copies:
        copy.wait()


def unpack_rest_kernel(w, query, back, query_sems, back_sems):
    width = query.shape[1]
    copies = []
    parts = query_sems.shape[0]
    rows = query.shape[0] // parts
    for i in range(parts):
        at = pl.ds(i * rows, rows)
        copies.append(
            pltpu.make_async_copy(
                w.at[at, pl.ds(2 * width, width)], query.at[at, :], query_sems.at[i]
            )
        )
    chips = back_sems.shape[0] // 2
    rows = back.shape[0] // chips
    for i in range(chips):
        for h in range(2):
            copies.append(
                pltpu.make_async_copy(
                    w.at[pl.ds((2 * i + h) * rows, rows), pl.ds(3 * width, width)],
                    back.at[pl.ds(i * rows, rows), pl.ds(h * width, width)],
                    back_sems.at[2 * i + h],
                )
            )
    for copy in copies:
        copy.start()
    for copy in copies:
        copy.wait()


def unpack(body, w, out_shape, sems):
    return pl.pallas_call(
        body,
        in_specs=[pl.BlockSpec(memory_space=pl.ANY)],
        out_specs=jax.tree.map(lambda _: pl.BlockSpec(memory_space=pltpu.VMEM), out_shape),
        out_shape=out_shape,
        scratch_shapes=[pltpu.SemaphoreType.DMA((count,)) for count in sems],
        compiler_params=pltpu.CompilerParams(vmem_limit_bytes=UNPACK_LIMIT),
    )(w)


def call(body, out_shape, flops, scalars, *operands):
    in_specs = [pl.BlockSpec(memory_space=pltpu.SMEM)]
    in_specs += [pl.BlockSpec(memory_space=pltpu.VMEM) for _ in operands]
    out_specs = jax.tree.map(lambda _: pl.BlockSpec(memory_space=pltpu.VMEM), out_shape)
    return pl.pallas_call(
        body,
        in_specs=in_specs,
        out_specs=out_specs,
        out_shape=out_shape,
        compiler_params=pltpu.CompilerParams(vmem_limit_bytes=VMEM_LIMIT),
        cost_estimate=pl.CostEstimate(flops=flops, bytes_accessed=1, transcendentals=0),
    )(scalars, *operands)


def pack_weights(core, w_qkv, w_out):
    shape = (w_qkv.shape[1], w_qkv.shape[2] * 2 // 3)
    return pl.pallas_call(
        pack_kernel,
        in_specs=[pl.BlockSpec(memory_space=pltpu.SMEM)]
        + [pl.BlockSpec(memory_space=pl.ANY)] * 2,
        out_specs=[pl.BlockSpec(memory_space=pltpu.VMEM)] * 2,
        out_shape=[jax.ShapeDtypeStruct(shape, BF16)] * 2,
        scratch_shapes=[
            pltpu.VMEM(w_qkv.shape, BF16),
            pltpu.VMEM(w_out.shape, BF16),
            pltpu.SemaphoreType.DMA((2,)),
        ],
        compiler_params=pltpu.CompilerParams(vmem_limit_bytes=PACK_LIMIT),
    )(core, w_qkv, w_out)


def join_weights(core, own, other):
    shape = (2 * own.shape[0], own.shape[1])
    return call(join_kernel, jax.ShapeDtypeStruct(shape, BF16), 1, core, own, other)


def project_early(scalars, own, w):
    rows, size = own.shape
    return call(
        early_kernel,
        jax.ShapeDtypeStruct((rows, w.shape[1]), F32),
        2 * rows * size * w.shape[1],
        scalars,
        own,
        w,
    )


def project_kv(scalars, acc, other, w):
    rows, width = acc.shape
    return call(
        kv_kernel,
        [
            jax.ShapeDtypeStruct((rows, width), BF16),
            jax.ShapeDtypeStruct((96, width), BF16),
            jax.ShapeDtypeStruct((32, width), BF16),
        ],
        2 * rows * other.shape[1] * width,
        scalars,
        acc,
        other,
        w,
    )


def attend_local(scalars, own, other, w, kv):
    rows = own.shape[0]
    width = w.shape[1]
    return call(
        local_kernel,
        [
            jax.ShapeDtypeStruct((rows, width), BF16),
            jax.ShapeDtypeStruct((rows, 2 * width), F32),
            jax.ShapeDtypeStruct((rows, HD), F32),
        ],
        4 * rows * (own.shape[1] + 2 * HD) * width,
        scalars,
        own,
        other,
        w,
        kv,
    )


def attend_remote(scalars, query, acc, stats, *sent):
    rows, width = query.shape
    return call(
        remote_kernel,
        jax.ShapeDtypeStruct((rows, width), BF16),
        4 * rows * 160 * width,
        scalars,
        query,
        acc,
        stats,
        *sent,
    )


def last_kernel(tick, scalars, acc, att_other, w, earlier, mine, theirs, result):
    core = scalars[0]
    rows = mine.shape[0]
    is_mine = scalars[scalars.shape[0] - 1] == tick

    @pl.when(is_mine)
    def _():
        part = acc[...] + dot(att_other[...], rows_of(1 - core, w))
        result[...] = part.astype(BF16)

    @pl.when(jnp.logical_not(is_mine))
    def _():
        result[...] = earlier[...]

    mine[...] = result[pl.ds(pl.multiple_of(core * rows, 16), rows), :]
    theirs[...] = result[pl.ds(pl.multiple_of((1 - core) * rows, 16), rows), :]


def project_last(scalars, tick, acc, att_other, w, earlier):
    rows, size = acc.shape
    return pl.pallas_call(
        functools.partial(last_kernel, tick),
        in_specs=[pl.BlockSpec(memory_space=pltpu.SMEM)]
        + [pl.BlockSpec(memory_space=pltpu.VMEM)] * 4,
        out_specs=[pl.BlockSpec(memory_space=pltpu.VMEM)] * 2,
        out_shape=[jax.ShapeDtypeStruct((rows // 2, size), BF16)] * 2,
        scratch_shapes=[pltpu.VMEM((rows, size), BF16)],
        compiler_params=pltpu.CompilerParams(vmem_limit_bytes=VMEM_LIMIT),
    )(scalars, acc, att_other, w, earlier)


def project_back_early(scalars, x_own, att_own, w):
    rows, size = x_own.shape
    return call(
        back_early_kernel,
        jax.ShapeDtypeStruct((rows, size), F32),
        2 * rows * size * att_own.shape[1],
        scalars,
        x_own,
        att_own,
        w,
    )


def project_back(scalars, tick, acc, att_other, w, earlier):
    rows, size = acc.shape
    return call(
        functools.partial(back_kernel, tick),
        [jax.ShapeDtypeStruct((rows, size), BF16)] * 2,
        2 * rows * size * att_other.shape[1],
        scalars,
        acc,
        att_other,
        w,
        earlier,
    )


def swap(value):
    count = lax.axis_size("seq")
    return lax.ppermute(value, "seq", [(i, i ^ 1) for i in range(count)])


def to_chips(value, moves):
    count = lax.axis_size("seq")
    step = 2 * GROUP_CHIPS
    pairs = [
        (first + 2 * source + core, first + 2 * target + core)
        for first in range(0, count, step)
        for source, target in moves
        for core in range(2)
    ]
    return lax.ppermute(value, "seq", pairs)


def in_order(core, own, other, axis):
    return jnp.where(
        core == 0,
        jnp.concatenate([own, other], axis=axis),
        jnp.concatenate([other, own], axis=axis),
    )


def gather_chips(block):
    count = lax.axis_size("seq")
    groups = [list(range(core, count, 2)) for core in range(2)]
    return lax.all_gather(block, "seq", axis=0, tiled=True, axis_index_groups=groups)


def local(tokens, w_qkv, w_out, offsets):
    section = lax.axis_index("section")
    section_count = lax.axis_size("section")
    seq = lax.axis_index("seq")
    core = seq % 2
    scalars = jnp.concatenate(
        [
            jnp.stack([core, (seq // 2) % GROUP_CHIPS]).astype(jnp.int32),
            offsets.reshape(-1).astype(jnp.int32),
            jnp.full((1,), section, jnp.int32),
        ]
    )
    with jax.named_scope("weights"):
        rows = w_qkv.shape[1]
        width = w_qkv.shape[2] // 6
        cut = w_out.shape[2] // 2
        core_array = jnp.full((1,), core, jnp.int32)
        own, other = pack_weights(core_array, w_qkv, w_out)
        block = join_weights(core_array, own, swap(other))
        block, tokens = lax.optimization_barrier((block, tokens))
        w_all = gather_chips(block)
        depth = w_all.shape[0]
        w_kv = unpack(
            unpack_kv_kernel, w_all, jax.ShapeDtypeStruct((depth, 2 * width), BF16), [8]
        )
        w_q, w_back = unpack(
            unpack_rest_kernel,
            w_all,
            [
                jax.ShapeDtypeStruct((depth, width), BF16),
                jax.ShapeDtypeStruct((depth // 2, cut), BF16),
            ],
            [8, depth // rows],
        )
    with jax.named_scope("tokens"):
        both = in_order(core, tokens[0], swap(tokens[0]), 0)
        left, right = both[:, :cut], both[:, cut:]
        x_own = jnp.where(core == 0, left, right)
        x_other = jnp.where(core == 0, right, left)
    result = x_own
    for tick in range(section_count):
        acc = project_early(scalars, x_own, w_kv)
        kv, send_pair, send = project_kv(scalars, acc, x_other, w_kv)
        cross = to_chips(send, ((0, 3), (1, 2)))
        mid = to_chips(send, ((0, 2), (1, 3)))
        pair = to_chips(send_pair, ((0, 1), (2, 3)))
        query, acc, stats = attend_local(scalars, x_own, x_other, w_q, kv)
        att = attend_remote(scalars, query, acc, stats, pair, mid, cross)
        acc = project_back_early(scalars, x_own, att, w_back)
        if tick + 1 < section_count:
            produced, result = project_back(scalars, tick, acc, swap(att), w_back, result)
        else:
            mine, theirs = project_last(scalars, tick, acc, swap(att), w_back, result)
        if tick + 1 < section_count:
            x_own = lax.ppermute(produced, "section", [(tick, tick + 1)])
            x_other = swap(x_own)
    with jax.named_scope("result"):
        theirs = swap(theirs)
        return in_order(core, mine, theirs, 1)[None, None]


def solution(mesh):
    return jax.shard_map(
        local,
        mesh=mesh,
        in_specs=(P(None, "seq", None), P("section", "seq", None), P("section", "seq", None), P()),
        out_specs=P("section", None, "seq", None),
        check_vma=False,
    )
```
